32 devices in a mesh: groups: 1, fsdp: 8 (over z, y), seq: 4 (over x, core), sub: 1.
Axes of the slice: x: 2, y: 2, z: 4, core: 2. Of those that a mesh axis runs over, the one named last changes fastest.
Arguments:
- tokens: bfloat16 [8, 1, 4, 128, 2048], P(('groups', 'fsdp'), 'sub', 'seq'), may hold values from -6 to 6
- frame_valid: int32 [8, 1, 4], P(('groups', 'fsdp'), 'sub'), may hold values from 0 to 1, as said below
- w_qkv: bfloat16 [2048, 3, 2048], P('fsdp', None, 'seq'), may hold values from -0.1875 to 0.1875
- w_out: bfloat16 [2048, 2048], P('seq', 'fsdp'), may hold values from -0.125 to 0.125
- w_act: bfloat16 [2048, 8192], P(None, 'fsdp'), may hold values from -0.125 to 0.125
- class_table: int32 [8192], P('fsdp'), may hold values from 0 to 120
- cam_bias: float32 [121], replicated, may hold values from -4 to 4
Outputs:
- hidden: bfloat16 [8, 1, 4, 128, 2048], P(('groups', 'fsdp'), 'sub', 'seq')
- logits: float32 [8, 1, 4, 8192], P('groups', 'sub', 'seq', 'fsdp')
The draws below stay inside these ranges and needn't reach their ends.
Inputs may be any that keep to these rules, and one draw needn't show every extreme that they name: `frame_valid`: each window has at least one frame with value 1.
All inputs are finite; a program needn't handle non-finite values.
Results may differ from the reference program's by a relative error of at most 0.0058.
Values may be sent and summed in bfloat16 or wider, within the bound.
No kernel may reach another device: no remote copies, remote signals or barrier semaphores. Data moves between devices by JAX's collectives and lax.ppermute only.
A program may use at most 128 MiB of HBM per device.

```python
import math
import jax
import jax.numpy as jnp
from jax import lax

D = 2048
H = 16
DH = 128
ACT = 8192
CAM = 121
FTOK = 128
FRAMES = 4
WF = 8
WS = 1


def draw_frame_valid(key, part):
    first_key, second_key = jax.random.split(jax.random.fold_in(key, 4711))
    coin_draw = jax.random.randint(first_key, (WF, WS, FRAMES), 0, 4)
    keep_flags = (coin_draw > 0).astype(jnp.int32)
    forced_frame = jax.random.randint(second_key, (WF, WS, 1), 0, FRAMES)
    frame_ids = jnp.arange(FRAMES, dtype=jnp.int32)[None, None, :]
    forced_flags = (frame_ids == forced_frame).astype(jnp.int32)
    return jnp.maximum(keep_flags, forced_flags)


def touch_ends(drawn, stream_key, least, top_value):
    place = [jax.random.randint(jax.random.fold_in(stream_key, axis), (), 0, length) for axis, length in enumerate(drawn.shape)]
    main_axis = drawn.shape.index(max(drawn.shape))
    beside = place[:main_axis] + [(place[main_axis] + 1) % drawn.shape[main_axis]] + place[main_axis + 1:]
    return drawn.at[tuple(place)].set(least).at[tuple(beside)].set(top_value)


def level_of(rng, shape, cuts, least, top_value):
    factor_of, own = 1.0, jax.random.fold_in(rng, 6)
    for dim, shards_of in cuts:
        draws = jnp.exp(jax.random.uniform(jax.random.fold_in(own, dim), (shards_of,), jnp.float32, least / len(cuts), top_value / len(cuts)))
        factor_of = factor_of * jnp.repeat(draws, shape[dim] // shards_of).reshape([-1 if axis == dim else 1 for axis in range(len(shape))])
    return factor_of


def bell_draw(key, dims, scale, reach, pieces=(), held_as=jnp.bfloat16):
    values = scale * jax.random.normal(key, dims, jnp.float32)
    if pieces:
        values = values * level_of(key, dims, pieces, -0.22, 0.18)
    return jnp.clip(values, -reach, reach).astype(held_as)


def setup_inputs(seed: int = 0, part: int = 0) -> dict:
    splits = jax.random.split(jax.random.key(seed), 8)
    own_keys = jax.random.split(jax.random.fold_in(splits[7], part), 8)
    tokens = bell_draw(own_keys[0], (WF, WS, FRAMES, FTOK, D), 1.0, 6.0, ((0, 8), (2, 4)))
    frame_valid = draw_frame_valid(jax.random.fold_in(jax.random.fold_in(splits[7], part), 71), part)
    w_qkv = bell_draw(splits[2], (D, 3, D), (D // 2) ** -0.5, 0.1875, ((0, 8), (2, 4)))
    w_out = bell_draw(splits[3], (D, D), D ** -0.5, 0.125, ((0, 4), (1, 8)))
    w_act = bell_draw(splits[4], (D, ACT), D ** -0.5, 0.125, ((1, 8),))
    class_table = touch_ends(jax.random.randint(splits[5], (ACT,), 0, CAM), jax.random.fold_in(splits[5], 1), 0, CAM - 1).astype(jnp.int32)
    cam_bias = bell_draw(splits[6], (CAM,), 1.0, 4.0, (), jnp.float32)
    return {"tokens": tokens, "frame_valid": frame_valid, "w_qkv": w_qkv, "w_out": w_out, "w_act": w_act, "class_table": class_table, "cam_bias": cam_bias}


def normalize(values):
    centre = lax.optimization_barrier(jnp.mean(values, axis=-1, keepdims=True))
    spread = lax.optimization_barrier(jnp.mean(jnp.square(values - centre), axis=-1, keepdims=True))
    return (values - centre) * lax.rsqrt(spread + 1e-05)

def reference(tokens, frame_valid, w_qkv, w_out, w_act, class_table, cam_bias):
    span_rows = FRAMES * FTOK
    flat_tokens = tokens.reshape(WF * WS, span_rows, D)
    flat_valid = frame_valid.reshape(WF * WS, FRAMES)
    weight_matrix = w_qkv.reshape(D, 3 * H * DH)
    score_scale = 1.0 / math.sqrt(DH)

    def one_window(window_pair):
        window_tokens, window_flags = window_pair
        normed = normalize(window_tokens.astype(jnp.float32)).astype(jnp.bfloat16)
        projected = jnp.dot(normed, weight_matrix, preferred_element_type=jnp.float32).astype(jnp.bfloat16)
        projected = lax.optimization_barrier(projected)
        projected = projected.reshape(span_rows, 3, H, DH).astype(jnp.float32)
        queries = projected[:, 0]
        keys_all = projected[:, 1]
        values_all = projected[:, 2]
        key_mask = jnp.repeat(window_flags.astype(jnp.float32), FTOK)
        scores = jnp.einsum('qhe,khe->hqk', queries, keys_all) * score_scale
        weights = jnp.exp(scores) * key_mask[None, None, :]
        totals = lax.optimization_barrier(jnp.sum(weights, axis=-1))
        rounded = lax.optimization_barrier(weights.astype(jnp.bfloat16)).astype(jnp.float32)
        mixed_heads = jnp.einsum('hqk,khe->hqe', rounded, values_all) / totals[:, :, None]
        mixed_heads = jnp.transpose(mixed_heads, (1, 0, 2)).reshape(span_rows, H * DH).astype(jnp.bfloat16)
        branch = jnp.dot(mixed_heads, w_out, preferred_element_type=jnp.float32)
        return (window_tokens.astype(jnp.float32) + branch).astype(jnp.bfloat16)
    hidden_flat = lax.map(one_window, (flat_tokens, flat_valid))
    hidden = hidden_flat.reshape(WF, WS, FRAMES, FTOK, D)
    hidden_wide = lax.optimization_barrier(hidden).astype(jnp.float32)
    pooled = normalize(lax.optimization_barrier(jnp.mean(hidden_wide, axis=3))).astype(jnp.bfloat16)
    pooled = pooled.reshape(WF * WS * FRAMES, D)
    head_scores = jnp.dot(pooled, w_act, preferred_element_type=jnp.float32)
    bias_cols = cam_bias[class_table]
    logits = (head_scores + bias_cols[None, :]).reshape(WF, WS, FRAMES, ACT)
    return (hidden, logits)
```

```python
import math

import jax
import jax.numpy as jnp
from jax import lax
from jax.sharding import PartitionSpec as P

DH = 128


def normalize(values):
    centre = jnp.mean(values, axis=-1, keepdims=True)
    spread = jnp.mean(jnp.square(values - centre), axis=-1, keepdims=True)
    return (values - centre) * lax.rsqrt(spread + 1e-05)


def ring_tables(n):
    order = list(range(0, n, 2)) + list(range(1, n, 2))[::-1]
    place = [order.index(i) for i in range(n)]
    forward = [(order[p], order[(p + 1) % n]) for p in range(n)]
    backward = [(b, a) for a, b in forward]
    return order, place, forward, backward


def ring_gather(blocks, n, forward, backward, split_dim):
    up = list(blocks)
    down = list(blocks)
    got = [{0: b} for b in blocks]
    for t in range(1, (n - 1) // 2 + 1):
        for i in range(len(blocks)):
            up[i] = lax.ppermute(up[i], "fsdp", forward)
            down[i] = lax.ppermute(down[i], "fsdp", backward)
            got[i][-t] = up[i]
            got[i][t] = down[i]
    if n % 2 == 0:
        for i in range(len(blocks)):
            half = blocks[i].shape[split_dim] // 2
            first = lax.slice_in_dim(up[i], 0, half, axis=split_dim)
            second = lax.slice_in_dim(down[i], half, 2 * half, axis=split_dim)
            first = lax.ppermute(first, "fsdp", forward)
            second = lax.ppermute(second, "fsdp", backward)
            got[i][n // 2] = jnp.concatenate([first, second], axis=split_dim)
    return got


def exchange(values, axis, size, bit):
    return lax.ppermute(values, axis, [(i, i ^ bit) for i in range(size)])


def make(mesh):
    fsdp = mesh.shape["fsdp"]
    seq = mesh.shape["seq"]
    order, place, forward, backward = ring_tables(fsdp)

    def per_device(tokens, frame_valid, w_qkv, w_out, w_act, class_table, cam_bias):
        frame_rows, width = tokens.shape[3], tokens.shape[4]
        me_f = lax.axis_index("fsdp")
        me_s = lax.axis_index("seq")
        my_place = jnp.array(place, jnp.int32)[me_f]
        order_t = jnp.array(order, jnp.int32)

        def owner(distance):
            return order_t[(my_place + distance) % fsdp]

        own = tokens[0, 0, 0].astype(jnp.float32)
        normed = normalize(own).astype(jnp.bfloat16)
        slots = normed[None]
        bit = 1
        while bit < seq:
            slots = jnp.concatenate([slots, exchange(slots, "seq", seq, bit)], axis=0)
            bit *= 2
        rows = slots.reshape(seq * frame_rows, width)
        frames = me_s ^ jnp.arange(seq, dtype=jnp.int32)
        valid = frame_valid[0, 0][frames].astype(jnp.float32)
        key_mask = jnp.repeat(valid, frame_rows)

        block = w_qkv.shape[0]
        parts = [w_qkv[:, c] for c in range(3)]
        got = ring_gather(parts, fsdp, forward, backward, 0)
        proj = []
        for c in range(3):
            total = None
            for d in got[c]:
                cols = lax.dynamic_slice_in_dim(rows, owner(d) * block, block, axis=1)
                term = jnp.dot(cols, got[c][d], preferred_element_type=jnp.float32)
                total = term if total is None else total + term
            proj.append(total.astype(jnp.bfloat16))
        heads = w_qkv.shape[2] // DH
        q, k, v = [p.reshape(p.shape[0], heads, DH) for p in proj]
        scores = jnp.einsum("qhe,khe->hqk", q, k, preferred_element_type=jnp.float32) * (
            1.0 / math.sqrt(DH)
        )
        weights = jnp.exp(scores) * key_mask[None, None, :]
        totals = jnp.sum(weights, axis=-1)
        mixed = jnp.einsum(
            "hqk,khe->qhe", weights.astype(jnp.bfloat16), v, preferred_element_type=jnp.float32
        )
        mixed = (mixed / jnp.transpose(totals)[:, :, None]).astype(jnp.bfloat16)
        mixed = mixed.reshape(rows.shape[0], heads * DH)

        last = (fsdp - 1) // 2
        w_out_late, _ = lax.optimization_barrier((w_out, got[0][last]))
        got_out = ring_gather([w_out_late], fsdp, forward, backward, 1)[0]

        cols_out = w_out.shape[1]
        hidden = jnp.zeros((frame_rows, width), jnp.bfloat16)
        pooled = jnp.zeros((width,), jnp.float32)
        names = sorted(got_out, key=abs)
        groups = [names[:3], names[3:5], names[5:]]
        for group in groups:
            if not group:
                continue
            w_group = jnp.concatenate([got_out[d] for d in group], axis=1)
            part = jnp.dot(mixed, w_group, preferred_element_type=jnp.float32)
            part = part.reshape(seq, frame_rows, w_group.shape[1])
            bit = 1
            while part.shape[0] > 1:
                pairs = part.reshape(part.shape[0] // 2, 2, frame_rows, part.shape[2])
                came = exchange(pairs[:, 1].astype(jnp.bfloat16), "seq", seq, bit)
                part = pairs[:, 0] + came.astype(jnp.float32)
                bit *= 2
            for j, d in enumerate(group):
                at = owner(d) * cols_out
                res = lax.dynamic_slice_in_dim(tokens[0, 0, 0], at, cols_out, axis=1)
                piece = res.astype(jnp.float32) + part[0][:, j * cols_out : (j + 1) * cols_out]
                piece = lax.optimization_barrier(piece.astype(jnp.bfloat16))
                hidden = lax.dynamic_update_slice_in_dim(hidden, piece, at, axis=1)
                mean = jnp.mean(piece.astype(jnp.float32), axis=0)
                pooled = lax.dynamic_update_slice_in_dim(pooled, mean, at, axis=0)

        pooled = normalize(pooled[None]).astype(jnp.bfloat16)
        bit = 1
        while bit < fsdp:
            pooled = jnp.concatenate([pooled, exchange(pooled, "fsdp", fsdp, bit)], axis=0)
            bit *= 2
        pooled = pooled[me_f ^ jnp.arange(fsdp, dtype=jnp.int32)]
        camera_ids = jnp.arange(cam_bias.shape[0], dtype=jnp.int32)
        onehot = (class_table[:, None] == camera_ids[None, :]).astype(jnp.float32)
        bias_cols = jnp.dot(onehot, cam_bias, precision=lax.Precision.HIGHEST)
        logits = jnp.dot(pooled, w_act, preferred_element_type=jnp.float32) + bias_cols[None, :]
        return (
            hidden.reshape(tokens.shape),
            logits.reshape(logits.shape[0], 1, 1, logits.shape[1]),
        )

    return per_device


def solution(mesh):
    in_specs = (
        P(("groups", "fsdp"), "sub", "seq", None, None),
        P(("groups", "fsdp"), "sub", None),
        P("fsdp", None, "seq"),
        P("seq", "fsdp"),
        P(None, "fsdp"),
        P("fsdp"),
        P(),
    )
    out_specs = (P(("groups", "fsdp"), "sub", "seq", None, None), P("groups", "sub", "seq", "fsdp"))
    return jax.shard_map(
        make(mesh), mesh=mesh, in_specs=in_specs, out_specs=out_specs, check_vma=False
    )
```

```python
import functools
import math

import jax
import jax.numpy as jnp
from jax import lax
from jax.experimental import pallas as pl
from jax.experimental.pallas import tpu as pltpu
from jax.sharding import PartitionSpec as P

DH = 128
LANES = 128
PAIR = 2
F32 = jnp.float32
BF16 = jnp.bfloat16
VMEM = pl.BlockSpec(memory_space=pltpu.VMEM)
SMEM = pl.BlockSpec(memory_space=pltpu.SMEM)
PARAMS = pltpu.CompilerParams(vmem_limit_bytes=40 * 2**20)


def normalize(values):
    centre = jnp.mean(values, axis=-1, keepdims=True)
    spread = jnp.mean(jnp.square(values - centre), axis=-1, keepdims=True)
    return (values - centre) * lax.rsqrt(spread + 1e-05)


def after(value, *done):
    return lax.optimization_barrier((value, *done))[0]


def cost(flops, size):
    return pl.CostEstimate(flops=flops, bytes_accessed=size, transcendentals=0)


def norm_kernel(order_ref, tokens_ref, normed_ref, mean_ref):
    values = tokens_ref[...].astype(F32)
    width = values.shape[1]
    centre = jnp.mean(values, axis=1, keepdims=True)
    spread = jnp.mean(jnp.square(values - centre), axis=1, keepdims=True)
    scale = lax.rsqrt(spread + 1e-05)
    mean_ref[...] = jnp.mean(values, axis=0, keepdims=True)
    count = order_ref.shape[0]
    block = width // count
    for i in range(count):
        at = pl.multiple_of(order_ref[i] * block, LANES)
        piece = tokens_ref[:, pl.ds(at, block)].astype(F32)
        normed_ref[:, i * block : (i + 1) * block] = ((piece - centre) * scale).astype(BF16)


def norm_call(order, tokens):
    rows, width = tokens.shape
    return pl.pallas_call(
        norm_kernel,
        out_shape=(
            jax.ShapeDtypeStruct((rows, width), BF16),
            jax.ShapeDtypeStruct((1, width), F32),
        ),
        in_specs=[SMEM, VMEM],
        out_specs=(VMEM, VMEM),
        compiler_params=PARAMS,
        cost_estimate=cost(8 * rows * width, 4 * rows * width),
        name="norm",
    )(order, tokens)


def project(rows, slots, swap):
    total = None
    block = slots[0].shape[0]
    for i, slot in enumerate(slots):
        j = i ^ 1 if swap else i
        term = jnp.dot(rows[:, j * block : (j + 1) * block], slot, preferred_element_type=F32)
        total = term if total is None else total + term
    return total.astype(BF16)


def slot_list(refs):
    return [ref[i] for ref in refs for i in range(ref.shape[0])]


def project_kernel(tensors, pieces, *refs):
    tokens = refs[:4]
    weights = refs[4 : 4 + tensors * pieces]
    outs = refs[4 + tensors * pieces :]
    for t in range(tensors):
        slots = slot_list(weights[t * pieces : (t + 1) * pieces])
        for w in range(2):
            half = 0
            for source, swap in ((tokens[w], False), (tokens[2 + w], True)):
                for frame in range(source.shape[0]):
                    rows = source.shape[1]
                    outs[t][w, half : half + rows, :] = project(source[frame], slots, swap)
                    half += rows


def project_call(tokens, weights):
    pieces = len(weights[0])
    rows = 2 * tokens[0].shape[0] * tokens[0].shape[1]
    columns = weights[0][0].shape[-1]
    depth = tokens[0].shape[2]
    flat = [w for tensor in weights for w in tensor]
    shape = jax.ShapeDtypeStruct((2, rows, columns), BF16)
    return pl.pallas_call(
        functools.partial(project_kernel, len(weights), pieces),
        out_shape=[shape] * len(weights),
        in_specs=[VMEM] * (4 + len(flat)),
        out_specs=[VMEM] * len(weights),
        compiler_params=PARAMS,
        cost_estimate=cost(4 * rows * columns * depth * len(weights), 4 * rows * depth),
        name="project",
    )(*tokens, *flat)


def attend_kernel(pieces, mask_ref, q_ref, k_ref, *refs):
    tokens = refs[:4]
    slots = slot_list(refs[4 : 4 + pieces])
    own_ref, pair_ref = refs[4 + pieces :]
    scale = 1.0 / math.sqrt(DH)
    for w, out in ((0, own_ref), (1, pair_ref)):
        parts = []
        for source, swap in ((tokens[w], False), (tokens[2 + w], True)):
            for frame in range(source.shape[0]):
                parts.append(project(source[frame], slots, swap))
        v = jnp.concatenate(parts, axis=0)
        for head in range(v.shape[1] // DH):
            at = slice(head * DH, (head + 1) * DH)
            scores = lax.dot_general(
                q_ref[w, :, at], k_ref[w, :, at], (((1,), (1,)), ((), ())), preferred_element_type=F32
            )
            weights = jnp.exp(scores * scale) * mask_ref[w]
            totals = jnp.sum(weights, axis=1, keepdims=True)
            mixed = jnp.dot(weights.astype(BF16), v[:, at], preferred_element_type=F32)
            out[:, at] = (mixed / totals).astype(BF16)


def attend_call(mask, q, k, tokens, v_slots):
    rows, columns = q.shape[1], q.shape[2]
    shape = jax.ShapeDtypeStruct((rows, columns), BF16)
    depth = tokens[0].shape[2]
    return pl.pallas_call(
        functools.partial(attend_kernel, len(v_slots)),
        out_shape=(shape, shape),
        in_specs=[VMEM] * (7 + len(v_slots)),
        out_specs=(VMEM, VMEM),
        compiler_params=PARAMS,
        cost_estimate=cost(4 * rows * columns * (depth + 2 * rows), 4 * rows * depth),
        name="attend",
    )(mask, q, k, *tokens, *v_slots)


def join_kernel(frames, flag_ref, own_ref, came_ref, mixed_ref, mean_ref):
    half = own_ref.shape[1]
    rows = own_ref.shape[0] // frames

    def write(first, second):
        for j, source in ((0, first), (1, second)):
            at = slice(j * half, (j + 1) * half)
            mixed_ref[:, at] = source[...]
            for frame in range(frames):
                part = source[frame * rows : (frame + 1) * rows, :].astype(F32)
                mean_ref[frame : frame + 1, at] = jnp.mean(part, axis=0, keepdims=True)

    @pl.when(flag_ref[0] == 0)
    def _():
        write(own_ref, came_ref)

    @pl.when(flag_ref[0] != 0)
    def _():
        write(came_ref, own_ref)


def join_call(flag, own, came, frames):
    rows, half = own.shape
    return pl.pallas_call(
        functools.partial(join_kernel, frames),
        out_shape=(
            jax.ShapeDtypeStruct((rows, 2 * half), BF16),
            jax.ShapeDtypeStruct((frames, 2 * half), F32),
        ),
        in_specs=[SMEM, VMEM, VMEM],
        out_specs=(VMEM, VMEM),
        compiler_params=PARAMS,
        cost_estimate=cost(4 * rows * half, 8 * rows * half),
        name="join",
    )(flag, own, came)


def times_block(values, parts):
    total, at = None, 0
    for part in parts:
        term = jnp.dot(values[:, at : at + part.shape[0]], part[...], preferred_element_type=F32)
        total = term if total is None else total + term
        at += part.shape[0]
    return total


def out_kernel(counts, mixed_ref, *refs):
    blocks, at = [], 0
    for count in counts:
        blocks.append(refs[at : at + count])
        at += count
    send_ref, keep_ref = refs[at:]
    half = mixed_ref.shape[0] // 2
    columns = blocks[0][0].shape[1]
    for i, parts in enumerate(blocks):
        result = times_block(mixed_ref, parts)
        keep_ref[:, i * columns : (i + 1) * columns] = result[:half]
        send_ref[:, i * columns : (i + 1) * columns] = result[half:].astype(BF16)


def out_call(mixed, blocks):
    flat = [part for parts in blocks for part in parts]
    rows, depth = mixed.shape
    columns = len(blocks) * blocks[0][0].shape[1]
    return pl.pallas_call(
        functools.partial(out_kernel, [len(parts) for parts in blocks]),
        out_shape=(
            jax.ShapeDtypeStruct((rows // 2, columns), BF16),
            jax.ShapeDtypeStruct((rows // 2, columns), F32),
        ),
        in_specs=[VMEM] * (1 + len(flat)),
        out_specs=(VMEM, VMEM),
        compiler_params=PARAMS,
        cost_estimate=cost(2 * rows * columns * depth, 2 * depth * columns + 6 * rows * columns),
        name="out",
    )(mixed, *flat)


def pool_kernel(counts, frames, means_ref, *refs):
    blocks, at = [], 0
    for count in counts:
        blocks.append(refs[at : at + count])
        at += count
    send_ref, keep_ref = refs[at:]
    rows = means_ref.shape[0]
    values = means_ref[...]
    upper = values.astype(BF16)
    lower = (values - upper.astype(F32)).astype(BF16)
    both = jnp.concatenate([upper, lower], axis=0)
    columns = blocks[0][0].shape[1]
    for i, parts in enumerate(blocks):
        result = times_block(both, parts)
        result = result[:rows] + result[rows:]
        keep_ref[:, i * columns : (i + 1) * columns] = result[: rows // 2]
        send_ref[:, i * columns : (i + 1) * columns] = result[rows // 2 :]


def pool_call(means, blocks, frames):
    flat = [part for parts in blocks for part in parts]
    rows, depth = means.shape
    columns = len(blocks) * blocks[0][0].shape[1]
    shape = jax.ShapeDtypeStruct((rows // 2, columns), F32)
    return pl.pallas_call(
        functools.partial(pool_kernel, [len(parts) for parts in blocks], frames),
        out_shape=(shape, shape),
        in_specs=[VMEM] * (1 + len(flat)),
        out_specs=(VMEM, VMEM),
        compiler_params=PARAMS,
        cost_estimate=cost(4 * rows * columns * depth, 2 * depth * columns),
        name="pool",
    )(means, *flat)


def finish_kernel(groups, owners_ref, tokens_ref, *refs):
    out_ref = refs[-1]
    rows = tokens_ref.shape[0]
    slot = 0
    block = tokens_ref.shape[1] // owners_ref.shape[0]
    for g in range(groups):
        sums, came = refs[2 * g], refs[2 * g + 1]
        for i in range(sums.shape[1] // block):
            at = pl.ds(pl.multiple_of(owners_ref[slot] * block, LANES), block)
            here = slice(i * block, (i + 1) * block)
            total = sums[:rows, here] + came[:, here].astype(F32)
            out_ref[:, at] = (tokens_ref[:, at].astype(F32) + total).astype(BF16)
            slot += 1


def finish_call(owners, tokens, sums):
    flat = [part for pair in sums for part in pair]
    return pl.pallas_call(
        functools.partial(finish_kernel, len(sums)),
        out_shape=jax.ShapeDtypeStruct(tokens.shape, BF16),
        in_specs=[SMEM, VMEM] + [VMEM] * len(flat),
        out_specs=VMEM,
        compiler_params=PARAMS,
        cost_estimate=cost(4 * tokens.size, 10 * tokens.size),
        name="finish",
    )(owners, tokens, *flat)


def head_kernel(owners_ref, windows_ref, sums_ref, came_ref, means_ref, act_ref, bias_ref, out_ref, pooled):
    count = owners_ref.shape[0]
    windows, width = means_ref.shape
    block = width // count
    for i in range(count):
        at = pl.ds(pl.multiple_of(owners_ref[i] * block, LANES), block)
        here = slice(i * block, (i + 1) * block)
        pooled[:, at] = sums_ref[:windows, here] + came_ref[:, here] + means_ref[:, at]
    values = normalize(pooled[...]).astype(BF16)
    logits = jnp.dot(values, act_ref[...], preferred_element_type=F32) + bias_ref[...]
    for i in range(windows):
        out_ref[pl.ds(windows_ref[i], 1), 0, 0, :] = logits[i : i + 1]


def head_call(owners, windows, sums, came, means, act, bias):
    columns = act.shape[1]
    return pl.pallas_call(
        head_kernel,
        out_shape=jax.ShapeDtypeStruct((means.shape[0], 1, 1, columns), F32),
        in_specs=[SMEM, SMEM] + [VMEM] * 5,
        out_specs=VMEM,
        scratch_shapes=[pltpu.VMEM(means.shape, F32)],
        compiler_params=PARAMS,
        cost_estimate=cost(2 * means.size * columns, 2 * act.size),
        name="head",
    )(owners, windows, sums, came, means, act, bias)


def ring_order(n):
    return list(range(0, n, 2)) + list(range(1, n, 2))[::-1]


def make(mesh):
    fsdp, seq = mesh.shape["fsdp"], mesh.shape["seq"]
    both = ("fsdp", "seq")
    order = ring_order(fsdp)
    place = [order.index(i) for i in range(fsdp)]
    forward = [(order[i], order[(i + 1) % fsdp]) for i in range(fsdp)]
    backward = [(b, a) for a, b in forward]
    wide_bits = [1 << i for i in range(1, (seq - 1).bit_length())]
    gather_bits = [1 << i for i in reversed(range((fsdp - 1).bit_length())) if (1 << i) != PAIR]

    def over_fsdp(value, bit):
        return lax.ppermute(value, "fsdp", [(i, i ^ bit) for i in range(fsdp)])

    def over_seq(value, bit):
        return lax.ppermute(value, "seq", [(i, i ^ bit) for i in range(seq)])

    def turn(value, k):
        pairs = []
        for f in range(fsdp):
            for s in range(seq):
                c, p = s & 1, (f // PAIR) & 1
                to_f = (f & ~PAIR) | (c * PAIR)
                to_s = (s & ~1) | (p ^ k)
                pairs.append((f * seq + s, to_f * seq + to_s))
        return lax.ppermute(value, both, pairs)

    def per_device(tokens, frame_valid, w_qkv, w_out, w_act, class_table, cam_bias):
        frame_rows, width = tokens.shape[3], tokens.shape[4]
        own_tokens = tokens.reshape(frame_rows, width)
        f, s = lax.axis_index("fsdp"), lax.axis_index("seq")
        core, parity = s & 1, (f // PAIR) & 1
        base = (f & ~PAIR) | (core * PAIR)
        half = w_qkv.shape[2] // 2
        block = w_qkv.shape[0]

        offsets = [0, PAIR]
        for bit in gather_bits:
            offsets = offsets + [o ^ bit for o in offsets]
        by_tensor = jnp.transpose(w_qkv, (1, 0, 2))

        def part(first, count, k):
            return lax.dynamic_slice(
                by_tensor, (first, 0, (parity ^ k) * half), (count, block, half)
            )

        q0, q1 = turn(part(0, 1, 0), 0), turn(part(0, 1, 1), 1)
        kv0, kv1 = turn(part(1, 2, 0), 0), turn(part(1, 2, 1), 1)
        first = [
            jnp.concatenate([q0, q1], axis=0),
            jnp.concatenate([kv0[:1], kv1[:1]], axis=0),
            jnp.concatenate([kv0[1:], kv1[1:]], axis=0),
        ]
        slots = []
        for start in first:
            held = [start]
            for bit in gather_bits:
                held = held + [over_fsdp(v, bit) for v in held]
            slots.append(held)

        columns = base ^ jnp.array(offsets, jnp.int32)
        normed, token_mean = norm_call(columns, own_tokens)
        own = normed[None]
        pair = over_fsdp(own, PAIR)
        for bit in wide_bits:
            own = jnp.concatenate([own, over_seq(own, bit)], axis=0)
            pair = jnp.concatenate([pair, over_seq(pair, bit)], axis=0)
        rows = (own, pair, over_seq(own, 1), over_seq(pair, 1))
        frame_slots = [0]
        for bit in wide_bits + [1]:
            frame_slots = frame_slots + [o ^ bit for o in frame_slots]
        frames = s ^ jnp.array(frame_slots, jnp.int32)
        valid = frame_valid[0, 0][frames].astype(F32)
        valid = jnp.stack([valid, over_fsdp(valid, PAIR)])
        mask = jnp.repeat(valid, frame_rows, axis=1)[:, None, :]

        q, k = project_call(rows, [slots[0], slots[1]])
        mixed_own, mixed_pair = attend_call(mask, q, k, rows, slots[2])
        came = over_fsdp(mixed_pair, PAIR)
        flag = (parity ^ core).reshape(1)
        mixed, frame_mean = join_call(flag, mixed_own, came, seq)

        rows_out = w_out.shape[0] // 2
        stay = lax.dynamic_slice_in_dim(w_out, core * rows_out, rows_out, axis=0)
        leave = lax.dynamic_slice_in_dim(w_out, (1 - core) * rows_out, rows_out, axis=0)
        start = jnp.concatenate([stay, over_seq(leave, 1)], axis=0)
        up = down = after(start, slots[1][-1])
        blocks, distance = [[start]], [0]
        for t in range(1, fsdp // 2):
            up = lax.ppermute(up, "fsdp", forward)
            down = lax.ppermute(down, "fsdp", backward)
            blocks += [[up], [down]]
            distance += [-t, t]
        blocks.append(
            [
                lax.ppermute(up[:rows_out], "fsdp", forward),
                lax.ppermute(down[rows_out:], "fsdp", backward),
            ]
        )
        distance.append(fsdp // 2)
        my_place = jnp.array(place, jnp.int32)[f]
        owners = jnp.array(order, jnp.int32)[(my_place + jnp.array(distance, jnp.int32)) % fsdp]

        means = jnp.concatenate([frame_mean, token_mean.reshape(seq, -1)], axis=0)[None]
        window_slots = [0]
        for bit in [1 << i for i in range((fsdp - 1).bit_length())]:
            means = jnp.concatenate([means, over_fsdp(means, bit)], axis=0)
            window_slots = window_slots + [o ^ bit for o in window_slots]
        windows = f ^ jnp.array(window_slots, jnp.int32)
        all_tokens = means[:, seq:].reshape(fsdp, width)
        all_frames = jnp.transpose(means[:, :seq], (1, 0, 2)).reshape(seq * fsdp, -1)

        def reduce_once(keep, arrived, to):
            total = keep + arrived.astype(F32)
            count = total.shape[0] // 2
            return total[:count], total[count:].astype(to)

        pool_send, pool_keep = pool_call(all_frames, blocks, seq)
        cuts = [blocks[:5], blocks[5:]] if len(blocks) > 5 else [blocks]
        sums = []
        arrived = over_seq(pool_send, 1)
        for bit in wide_bits[::-1]:
            pool_keep, leave = reduce_once(pool_keep, arrived, F32)
            arrived = over_seq(leave, bit)
        pool_came = arrived
        for cut in cuts:
            send, keep = out_call(mixed, cut)
            arrived = over_seq(send, 1)
            for bit in wide_bits[::-1]:
                keep, leave = reduce_once(keep, arrived, BF16)
                arrived = over_seq(leave, bit)
            sums.append((keep, arrived))
        hidden = finish_call(owners, own_tokens, sums)

        camera_ids = jnp.arange(cam_bias.shape[0], dtype=jnp.int32)
        onehot = (class_table[:, None] == camera_ids[None, :]).astype(F32)
        bias = jnp.dot(onehot, cam_bias, precision=lax.Precision.HIGHEST)[None]
        logits = head_call(owners, windows, pool_keep, pool_came, all_tokens, w_act, bias)
        return hidden.reshape(tokens.shape), logits

    return per_device


def plain(tokens, frame_valid, w_qkv, w_out, w_act, class_table, cam_bias):
    windows_here, frame_rows, width = tokens.shape[0], tokens.shape[3], tokens.shape[4]
    own_rows = tokens[:, 0, 0].astype(F32)
    normed = normalize(own_rows).astype(BF16)
    gathered = lax.all_gather(normed[:, None], "seq", axis=1, tiled=True)
    frame_count = gathered.shape[1]
    span = frame_count * frame_rows
    rows = gathered.reshape(windows_here, span, width)
    full_qkv = lax.all_gather(w_qkv, "fsdp", axis=0, tiled=True)
    projected = jnp.einsum("wsd,dcn->wscn", rows, full_qkv, preferred_element_type=F32)
    heads = full_qkv.shape[2] // DH
    projected = projected.astype(BF16).reshape(windows_here, span, 3, heads, DH)
    q, k, v = projected[:, :, 0], projected[:, :, 1], projected[:, :, 2]
    key_mask = jnp.repeat(frame_valid[:, 0].astype(F32), frame_rows, axis=1)
    scores = jnp.einsum("wqhe,wkhe->whqk", q, k, preferred_element_type=F32) / math.sqrt(DH)
    weights = jnp.exp(scores) * key_mask[:, None, None, :]
    totals = jnp.sum(weights, axis=-1)
    mixed = jnp.einsum("whqk,wkhe->wqhe", weights.astype(BF16), v, preferred_element_type=F32)
    mixed = (mixed / jnp.transpose(totals, (0, 2, 1))[:, :, :, None]).astype(BF16)
    mixed = mixed.reshape(windows_here, frame_count, frame_rows, heads * DH)
    mixed = jnp.transpose(mixed, (1, 0, 2, 3)).reshape(-1, heads * DH)
    full_out = lax.all_gather(w_out, "fsdp", axis=1, tiled=True)
    branch = lax.psum_scatter(
        jnp.dot(mixed, full_out, preferred_element_type=F32), "seq", scatter_dimension=0, tiled=True
    )
    hidden = (own_rows + branch.reshape(windows_here, frame_rows, width)).astype(BF16)
    wide = lax.optimization_barrier(hidden).astype(F32)
    pooled = normalize(jnp.mean(wide, axis=1)).astype(BF16)
    camera_ids = jnp.arange(cam_bias.shape[0], dtype=jnp.int32)
    onehot = (class_table[:, None] == camera_ids[None, :]).astype(F32)
    bias = jnp.dot(onehot, cam_bias, precision=lax.Precision.HIGHEST)
    everywhere = lax.all_gather(pooled, "fsdp", axis=0, tiled=True)
    logits = jnp.dot(everywhere, w_act, preferred_element_type=F32) + bias[None, :]
    return (
        hidden.reshape(windows_here, 1, 1, frame_rows, width),
        logits.reshape(logits.shape[0], 1, 1, logits.shape[1]),
    )


def solution(mesh):
    fsdp, seq = mesh.shape["fsdp"], mesh.shape["seq"]

    def whole(tokens, frame_valid, w_qkv, w_out, w_act, class_table, cam_bias):
        args = (tokens, frame_valid, w_qkv, w_out, w_act, class_table, cam_bias)
        powers = all(n & (n - 1) == 0 for n in (fsdp, seq)) and fsdp >= 4 and seq >= 2
        aligned = w_qkv.shape[0] % (fsdp * LANES) == 0 and w_qkv.shape[2] % (seq * 2 * DH) == 0
        one_window = tokens.shape[0] == mesh.shape["groups"] * fsdp
        one_window = one_window and tokens.shape[1] == mesh.shape["sub"] and tokens.shape[2] == seq
        one = make(mesh) if powers and aligned and one_window else plain
        in_specs = (
            P(("groups", "fsdp"), "sub", "seq", None, None),
            P(("groups", "fsdp"), "sub", None),
            P("fsdp", None, "seq"),
            P("seq", "fsdp"),
            P(None, "fsdp"),
            P("fsdp"),
            P(),
        )
        out_specs = (
            P(("groups", "fsdp"), "sub", "seq", None, None),
            P("groups", "sub", "seq", "fsdp"),
        )
        run = jax.shard_map(
            one, mesh=mesh, in_specs=in_specs, out_specs=out_specs, check_vma=False
        )
        return run(*args)

    return whole
```

```python
import functools
import math

import jax
import jax.numpy as jnp
from jax import lax
from jax.experimental import pallas as pl
from jax.experimental.pallas import tpu as pltpu
from jax.sharding import PartitionSpec as P

DH = 128
LANES = 128
F32 = jnp.float32
BF16 = jnp.bfloat16
VMEM = pl.BlockSpec(memory_space=pltpu.VMEM)
SMEM = pl.BlockSpec(memory_space=pltpu.SMEM)
PARAMS = pltpu.CompilerParams(vmem_limit_bytes=16 * 2**20)


def normalize(values):
    centre = jnp.mean(values, axis=-1, keepdims=True)
    spread = jnp.mean(jnp.square(values - centre), axis=-1, keepdims=True)
    return (values - centre) * lax.rsqrt(spread + 1e-05)


def after(value, *done):
    return lax.optimization_barrier((value, *done))[0]


def cost(flops, size):
    return pl.CostEstimate(flops=flops, bytes_accessed=size, transcendentals=0)


def ring_place(index, n):
    return index // 2 if index % 2 == 0 else n - 1 - index // 2


def owners(distances):
    n = len(distances)
    me = lax.axis_index("fsdp")
    half = lax.shift_right_logical(me, 1)
    place = jnp.where((me & 1) == 0, half, n - 1 - half)
    found = []
    for distance in distances:
        at = lax.rem(place + (distance + n), n)
        found.append(jnp.where(at < n // 2, 2 * at, 2 * (n - at) - 1))
    return found


def norm_kernel(distances, tokens_ref, normed_ref, mean_ref):
    values = tokens_ref[...].astype(F32)
    width = values.shape[1]
    centre = jnp.mean(values, axis=1, keepdims=True)
    spread = jnp.mean(jnp.square(values - centre), axis=1, keepdims=True)
    scale = lax.rsqrt(spread + 1e-05)
    mean = jnp.mean(values, axis=0, keepdims=True)
    columns = mean_ref.shape[1]
    for i in range(mean_ref.shape[0]):
        mean_ref[i : i + 1, :] = mean[:, i * columns : (i + 1) * columns]
    block = width // len(distances)
    for i, owner in enumerate(owners(distances)):
        at = pl.multiple_of(owner * block, LANES)
        piece = tokens_ref[:, pl.ds(at, block)].astype(F32)
        normed_ref[:, i * block : (i + 1) * block] = ((piece - centre) * scale).astype(BF16)


def norm_call(distances, tokens, columns):
    rows, width = tokens.shape
    return pl.pallas_call(
        functools.partial(norm_kernel, distances),
        out_shape=(
            jax.ShapeDtypeStruct((rows, width), BF16),
            jax.ShapeDtypeStruct((width // columns, columns), F32),
        ),
        in_specs=[VMEM],
        out_specs=(VMEM, VMEM),
        compiler_params=PARAMS,
        cost_estimate=cost(8 * rows * width, 4 * rows * width),
        name="norm",
    )(tokens)


def fetch(sources, buffers, sems):
    copies = [
        pltpu.make_async_copy(source, buffer, sems.at[i])
        for i, (source, buffer) in enumerate(zip(sources, buffers))
    ]
    for copy in copies:
        copy.start()

    def get(i):
        copies[i].wait()
        return buffers[i][...]

    return get


def frames_of(refs):
    return [(ref, frame) for ref in refs for frame in range(ref.shape[0])]


def times_rows(sources, first, blocks, total):
    at = first
    for block in blocks:
        depth = block.shape[0]
        rows = [ref[frame, :, at : at + depth] for ref, frame in frames_of(sources)]
        term = jnp.dot(jnp.concatenate(rows, axis=0), block, preferred_element_type=F32)
        total = term if total is None else total + term
        at += depth
    return total


def early_kernel(tensors, own_ref, core_ref, *refs):
    count = (len(refs) - 2) // 2
    sources, out_ref = refs[:count], refs[count]
    buffers, sems = refs[count + 1 : -1], refs[-1]
    get = fetch(sources, buffers, sems)
    for tensor in range(tensors):
        blocks = [get(i) for i in range(tensor, count, tensors)]
        out_ref[tensor] = times_rows((own_ref, core_ref), 0, blocks, None)


ANY = pl.BlockSpec(memory_space=pltpu.HBM)


def scratch_for(blocks):
    return [pltpu.VMEM(b.shape, b.dtype) for b in blocks] + [pltpu.SemaphoreType.DMA((len(blocks),))]


def early_call(tokens, blocks, tensors):
    rows = 2 * tokens[0].shape[0] * tokens[0].shape[1]
    columns = blocks[0].shape[1]
    depth = sum(b.shape[0] for b in blocks)
    return pl.pallas_call(
        functools.partial(early_kernel, tensors),
        out_shape=jax.ShapeDtypeStruct((tensors, rows, columns), F32),
        in_specs=[VMEM] * 2 + [ANY] * len(blocks),
        out_specs=VMEM,
        scratch_shapes=scratch_for(blocks),
        compiler_params=PARAMS,
        cost_estimate=cost(2 * rows * columns * depth, 2 * columns * depth),
        name="early",
    )(*tokens, *blocks)


def late_kernel(counts, first, own_ref, core_ref, part_ref, *refs):
    count = sum(counts)
    sources, outs = refs[:count], refs[count : count + len(counts)]
    buffers, sems = refs[count + len(counts) : -1], refs[-1]
    get = fetch(sources, buffers, sems)
    at = 0
    for tensor, number in enumerate(counts):
        blocks = [get(at + i) for i in range(number)]
        at += number
        total = times_rows((own_ref, core_ref), first, blocks, part_ref[tensor])
        outs[tensor][...] = total.astype(BF16)


def late_call(tokens, part, blocks):
    flat = [b for tensor in blocks for b in tensor]
    rows, columns = part.shape[1], part.shape[2]
    depth = sum(b.shape[0] for b in flat)
    first = tokens[0].shape[2] - sum(b.shape[0] for b in blocks[0])
    shape = jax.ShapeDtypeStruct((rows, columns), BF16)
    return pl.pallas_call(
        functools.partial(late_kernel, [len(b) for b in blocks], first),
        out_shape=[shape] * len(blocks),
        in_specs=[VMEM] * 3 + [ANY] * len(flat),
        out_specs=[VMEM] * len(blocks),
        scratch_shapes=scratch_for(flat),
        compiler_params=PARAMS,
        cost_estimate=cost(2 * rows * columns * depth, 2 * columns * depth),
        name="late",
    )(*tokens, part, *flat)


def attend_kernel(first, slots, valid_ref, mean_ref, own_ref, core_ref, part_ref, q_ref, k_ref, *refs):
    count = (len(refs) - 3) // 2
    mixed_ref, means_ref = refs[count : count + 2]
    get = fetch(refs[:count], refs[count + 2 : -1], refs[-1])
    scale = 1.0 / math.sqrt(DH)
    rows = own_ref.shape[1]
    frames = mixed_ref.shape[0] // rows
    means_ref[0, frames:, :] = mean_ref[...]
    me = lax.axis_index("seq")
    flags = [valid_ref[me ^ slot].astype(F32) for slot in slots]
    mask = jnp.concatenate([jnp.full((1, rows), flag, F32) for flag in flags], axis=1)
    blocks = [get(i) for i in range(count)]
    v = times_rows((own_ref, core_ref), first, blocks, part_ref[part_ref.shape[0] - 1]).astype(BF16)
    for head in range(v.shape[1] // DH):
        at = slice(head * DH, (head + 1) * DH)
        scores = lax.dot_general(
            q_ref[:, at], k_ref[:, at], (((1,), (1,)), ((), ())), preferred_element_type=F32
        )
        weights = jnp.exp(scores * scale) * mask
        totals = jnp.sum(weights, axis=1, keepdims=True)
        mixed = jnp.dot(weights.astype(BF16), v[:, at], preferred_element_type=F32)
        mixed = (mixed / totals).astype(BF16)
        mixed_ref[:, at] = mixed
        for frame in range(frames):
            part = mixed[frame * rows : (frame + 1) * rows].astype(F32)
            means_ref[0, frame : frame + 1, at] = jnp.mean(part, axis=0, keepdims=True)


def attend_call(slots, valid, token_mean, tokens, part, q, k, blocks):
    rows, columns = q.shape
    depth = tokens[0].shape[2]
    means = rows // tokens[0].shape[1] + token_mean.shape[0]
    first = depth - sum(b.shape[0] for b in blocks)
    return pl.pallas_call(
        functools.partial(attend_kernel, first, slots),
        out_shape=(
            jax.ShapeDtypeStruct((rows, columns), BF16),
            jax.ShapeDtypeStruct((1, means, columns), F32),
        ),
        in_specs=[SMEM] + [VMEM] * 6 + [ANY] * len(blocks),
        out_specs=(VMEM, VMEM),
        scratch_shapes=scratch_for(blocks),
        compiler_params=PARAMS,
        cost_estimate=cost(2 * rows * columns * (depth + 2 * rows), 2 * columns * depth),
        name="attend",
    )(valid, token_mean, *tokens, part, q, k, *blocks)


def times_block(values, parts):
    total, at = None, 0
    for part in parts:
        term = jnp.dot(values[:, at : at + part.shape[0]], part[...], preferred_element_type=F32)
        total = term if total is None else total + term
        at += part.shape[0]
    return total


def out_kernel(counts, mixed_ref, *refs):
    blocks, at = [], 0
    for count in counts:
        blocks.append(refs[at : at + count])
        at += count
    send_ref, keep_ref = refs[at:]
    half = mixed_ref.shape[0] // 2
    columns = blocks[0][0].shape[1]
    for i, parts in enumerate(blocks):
        result = times_block(mixed_ref, parts)
        keep_ref[:, i * columns : (i + 1) * columns] = result[:half]
        send_ref[:, i * columns : (i + 1) * columns] = result[half:].astype(BF16)


def out_call(mixed, blocks):
    flat = [part for parts in blocks for part in parts]
    rows, depth = mixed.shape
    columns = len(blocks) * blocks[0][0].shape[1]
    return pl.pallas_call(
        functools.partial(out_kernel, [len(parts) for parts in blocks]),
        out_shape=(
            jax.ShapeDtypeStruct((rows // 2, columns), BF16),
            jax.ShapeDtypeStruct((rows // 2, columns), F32),
        ),
        in_specs=[VMEM] * (1 + len(flat)),
        out_specs=(VMEM, VMEM),
        compiler_params=PARAMS,
        cost_estimate=cost(2 * rows * columns * depth, 2 * depth * columns + 6 * rows * columns),
        name="out",
    )(mixed, *flat)


def pool_kernel(counts, frames, means_ref, *refs):
    blocks, at = [], 0
    for count in counts:
        blocks.append(refs[at : at + count])
        at += count
    send_ref, keep_ref, held = refs[at:]
    windows = means_ref.shape[0]
    rows = windows * frames
    for r in range(windows):
        for frame in range(frames):
            to = frame * windows + r
            held[to : to + 1, :] = means_ref[r, frame : frame + 1, :]
    values = held[...]
    upper = values.astype(BF16)
    lower = (values - upper.astype(F32)).astype(BF16)
    both = jnp.concatenate([upper, lower], axis=0)
    columns = blocks[0][0].shape[1]
    for i, parts in enumerate(blocks):
        result = times_block(both, parts)
        result = result[:rows] + result[rows:]
        keep_ref[:, i * columns : (i + 1) * columns] = result[: rows // 2]
        send_ref[:, i * columns : (i + 1) * columns] = result[rows // 2 :]


def pool_call(means, blocks, frames):
    flat = [part for parts in blocks for part in parts]
    rows, depth = frames * means.shape[0], means.shape[2]
    columns = len(blocks) * blocks[0][0].shape[1]
    shape = jax.ShapeDtypeStruct((rows // 2, columns), F32)
    return pl.pallas_call(
        functools.partial(pool_kernel, [len(parts) for parts in blocks], frames),
        out_shape=(shape, shape),
        in_specs=[VMEM] * (1 + len(flat)),
        out_specs=(VMEM, VMEM),
        scratch_shapes=[pltpu.VMEM((rows, depth), F32)],
        compiler_params=PARAMS,
        cost_estimate=cost(4 * rows * columns * depth, 2 * depth * columns),
        name="pool",
    )(means, *flat)


def finish_kernel(distances, groups, tokens_ref, *refs):
    out_ref = refs[-1]
    rows = tokens_ref.shape[0]
    slot = 0
    block = tokens_ref.shape[1] // len(distances)
    found = owners(distances)
    for g in range(groups):
        sums, came = refs[2 * g], refs[2 * g + 1]
        for i in range(sums.shape[1] // block):
            at = pl.ds(pl.multiple_of(found[slot] * block, LANES), block)
            here = slice(i * block, (i + 1) * block)
            total = sums[:rows, here] + came[:, here].astype(F32)
            out_ref[:, at] = (tokens_ref[:, at].astype(F32) + total).astype(BF16)
            slot += 1


def finish_call(distances, tokens, sums):
    flat = [part for pair in sums for part in pair]
    return pl.pallas_call(
        functools.partial(finish_kernel, distances, len(sums)),
        out_shape=jax.ShapeDtypeStruct(tokens.shape, BF16),
        in_specs=[VMEM] * (1 + len(flat)),
        out_specs=VMEM,
        compiler_params=PARAMS,
        cost_estimate=cost(4 * tokens.size, 10 * tokens.size),
        name="finish",
    )(tokens, *flat)


def head_kernel(distances, sums_ref, came_ref, means_ref, act_ref, bias_ref, out_ref, pooled):
    windows, width = pooled.shape
    columns = means_ref.shape[2]
    first = means_ref.shape[1] - width // columns
    for i in range(width // columns):
        pooled[:, i * columns : (i + 1) * columns] = means_ref[:, first + i, :]
    block = width // len(distances)
    for i, owner in enumerate(owners(distances)):
        at = pl.ds(pl.multiple_of(owner * block, LANES), block)
        here = slice(i * block, (i + 1) * block)
        pooled[:, at] += sums_ref[:windows, here] + came_ref[:, here]
    values = normalize(pooled[...]).astype(BF16)
    logits = jnp.dot(values, act_ref[...], preferred_element_type=F32) + bias_ref[...]
    me = lax.axis_index("fsdp")
    for i in range(windows):
        out_ref[pl.ds(me ^ i, 1), 0, 0, :] = logits[i : i + 1]


def head_call(distances, sums, came, means, act, bias):
    width, columns = act.shape
    return pl.pallas_call(
        functools.partial(head_kernel, distances),
        out_shape=jax.ShapeDtypeStruct((means.shape[0], 1, 1, columns), F32),
        in_specs=[VMEM] * 5,
        out_specs=VMEM,
        scratch_shapes=[pltpu.VMEM((means.shape[0], width), F32)],
        compiler_params=PARAMS,
        cost_estimate=cost(2 * means.shape[0] * act.size, 2 * act.size),
        name="head",
    )(sums, came, means, act, bias)


def make(mesh):
    fsdp, seq = mesh.shape["fsdp"], mesh.shape["seq"]
    order = sorted(range(fsdp), key=lambda i: ring_place(i, fsdp))
    forward = [(order[i], order[(i + 1) % fsdp]) for i in range(fsdp)]
    backward = [(b, a) for a, b in forward]
    wide_bits = [1 << i for i in range(1, (seq - 1).bit_length())]
    distances = [0]
    for t in range(1, fsdp // 2):
        distances += [-t, t]
    distances.append(fsdp // 2)

    def over_fsdp(value, bit):
        return lax.ppermute(value, "fsdp", [(i, i ^ bit) for i in range(fsdp)])

    def over_seq(value, bit):
        return lax.ppermute(value, "seq", [(i, i ^ bit) for i in range(seq)])

    def ring_step(held):
        blocks, up, down = held
        up = lax.ppermute(up, "fsdp", forward)
        down = lax.ppermute(down, "fsdp", backward)
        return blocks + [up, down], up, down

    def ring_last(held, upwards):
        blocks, up, down = held
        if upwards:
            return blocks + [lax.ppermute(up, "fsdp", forward)]
        return blocks + [lax.ppermute(down, "fsdp", backward)]

    def gate(held, *done):
        blocks, up, down = held
        return blocks, after(up, *done), after(down, *done)

    def per_device(tokens, frame_valid, w_qkv, w_out, w_act, class_table, cam_bias):
        frame_rows, width = tokens.shape[3], tokens.shape[4]
        own_tokens = tokens.reshape(frame_rows, width)
        by_tensor = jnp.transpose(w_qkv, (1, 0, 2))
        steps = fsdp // 2
        rings = [ring_step(([part], part, part)) for part in by_tensor]

        normed, token_mean = norm_call(
            distances, own_tokens, w_qkv.shape[2]
        )
        own = normed[None]
        frame_slots = [0]
        for bit in wide_bits:
            own = jnp.concatenate([own, over_seq(own, bit)], axis=0)
            frame_slots = frame_slots + [o ^ bit for o in frame_slots]
        frame_slots = frame_slots + [o ^ 1 for o in frame_slots]

        soon = 2 if steps > 2 else 1
        for _ in range(1, soon):
            rings = [ring_step(held) for held in rings]
        rows = (own, over_seq(after(own, rings[0][1], rings[0][2]), 1))
        count = 2 * soon + 1
        part = early_call(rows, [held[0][i] for i in range(count) for held in rings], len(rings))
        start = after(w_out, rings[2][1], rings[2][2])
        out = ([start], start, start)
        for i in range(soon, steps - 1):
            rings = [ring_step(held) for held in rings]
            out = ring_step(out)
        out = gate(out, *rings[2][1:])
        qkv = [ring_last(held, upwards) for held, upwards in zip(rings, (True, False, True))]
        while len(out[0]) < 2 * steps - 1:
            out = ring_step(out)
        blocks = [[block] for block in ring_last(out, False)]

        q, k = late_call(rows, part, [qkv[0][count:], qkv[1][count:]])
        mixed, means = attend_call(
            frame_slots, frame_valid.reshape(seq), token_mean, rows, part, q, k, qkv[2][count:]
        )

        cut = len(blocks) - 1
        send, keep = out_call(mixed, blocks[:cut])
        came = over_seq(send, 1)
        bits = [1 << i for i in range((fsdp - 1).bit_length())]
        for bit in bits:
            means = after(means, came) if bit == bits[-1] else means
            means = jnp.concatenate([means, over_fsdp(means, bit)], axis=0)

        def reduce_once(keep, arrived, to):
            total = keep + arrived.astype(F32)
            count = total.shape[0] // 2
            return total[:count], total[count:].astype(to)

        def reduce_all(send, keep, to, arrived=None):
            arrived = over_seq(send, 1) if arrived is None else arrived
            for bit in wide_bits[::-1]:
                keep, leave = reduce_once(keep, arrived, to)
                arrived = over_seq(leave, bit)
            return keep, arrived

        early = reduce_all(send, keep, BF16, came)
        pool_keep, pool_came = reduce_all(*pool_call(after(means, early[1]), blocks, seq), F32)
        sums = [early, reduce_all(*out_call(after(mixed, means), blocks[cut:]), BF16)]
        hidden = finish_call(distances, own_tokens, sums)

        camera_ids = jnp.arange(cam_bias.shape[0], dtype=jnp.int32)
        onehot = (class_table[:, None] == camera_ids[None, :]).astype(F32)
        bias = jnp.dot(onehot, cam_bias, precision=lax.Precision.HIGHEST)[None]
        logits = head_call(distances, pool_keep, pool_came, means, w_act, bias)
        return hidden.reshape(tokens.shape), logits

    return per_device


def plain(tokens, frame_valid, w_qkv, w_out, w_act, class_table, cam_bias):
    windows_here, frame_rows, width = tokens.shape[0], tokens.shape[3], tokens.shape[4]
    own_rows = tokens[:, 0, 0].astype(F32)
    normed = normalize(own_rows).astype(BF16)
    gathered = lax.all_gather(normed[:, None], "seq", axis=1, tiled=True)
    frame_count = gathered.shape[1]
    span = frame_count * frame_rows
    rows = gathered.reshape(windows_here, span, width)
    full_qkv = lax.all_gather(w_qkv, "fsdp", axis=0, tiled=True)
    projected = jnp.einsum("wsd,dcn->wscn", rows, full_qkv, preferred_element_type=F32)
    heads = full_qkv.shape[2] // DH
    projected = projected.astype(BF16).reshape(windows_here, span, 3, heads, DH)
    q, k, v = projected[:, :, 0], projected[:, :, 1], projected[:, :, 2]
    key_mask = jnp.repeat(frame_valid[:, 0].astype(F32), frame_rows, axis=1)
    scores = jnp.einsum("wqhe,wkhe->whqk", q, k, preferred_element_type=F32) / math.sqrt(DH)
    weights = jnp.exp(scores) * key_mask[:, None, None, :]
    totals = jnp.sum(weights, axis=-1)
    mixed = jnp.einsum("whqk,wkhe->wqhe", weights.astype(BF16), v, preferred_element_type=F32)
    mixed = (mixed / jnp.transpose(totals, (0, 2, 1))[:, :, :, None]).astype(BF16)
    mixed = mixed.reshape(windows_here, frame_count, frame_rows, heads * DH)
    mixed = jnp.transpose(mixed, (1, 0, 2, 3)).reshape(-1, heads * DH)
    full_out = lax.all_gather(w_out, "fsdp", axis=1, tiled=True)
    branch = lax.psum_scatter(
        jnp.dot(mixed, full_out, preferred_element_type=F32), "seq", scatter_dimension=0, tiled=True
    )
    hidden = (own_rows + branch.reshape(windows_here, frame_rows, width)).astype(BF16)
    wide = lax.optimization_barrier(hidden).astype(F32)
    pooled = normalize(jnp.mean(wide, axis=1)).astype(BF16)
    camera_ids = jnp.arange(cam_bias.shape[0], dtype=jnp.int32)
    onehot = (class_table[:, None] == camera_ids[None, :]).astype(F32)
    bias = jnp.dot(onehot, cam_bias, precision=lax.Precision.HIGHEST)
    everywhere = lax.all_gather(pooled, "fsdp", axis=0, tiled=True)
    logits = jnp.dot(everywhere, w_act, preferred_element_type=F32) + bias[None, :]
    return (
        hidden.reshape(windows_here, 1, 1, frame_rows, width),
        logits.reshape(logits.shape[0], 1, 1, logits.shape[1]),
    )


def solution(mesh):
    fsdp, seq = mesh.shape["fsdp"], mesh.shape["seq"]

    def whole(tokens, frame_valid, w_qkv, w_out, w_act, class_table, cam_bias):
        args = (tokens, frame_valid, w_qkv, w_out, w_act, class_table, cam_bias)
        powers = all(n & (n - 1) == 0 for n in (fsdp, seq)) and fsdp >= 4 and seq >= 2
        aligned = w_qkv.shape[0] % (fsdp * LANES) == 0 and w_qkv.shape[2] % (seq * 2 * DH) == 0
        one_window = tokens.shape[0] == mesh.shape["groups"] * fsdp
        one_window = one_window and tokens.shape[1] == mesh.shape["sub"] and tokens.shape[2] == seq
        one = make(mesh) if powers and aligned and one_window else plain
        in_specs = (
            P(("groups", "fsdp"), "sub", "seq", None, None),
            P(("groups", "fsdp"), "sub", None),
            P("fsdp", None, "seq"),
            P("seq", "fsdp"),
            P(None, "fsdp"),
            P("fsdp"),
            P(),
        )
        out_specs = (
            P(("groups", "fsdp"), "sub", "seq", None, None),
            P("groups", "sub", "seq", "fsdp"),
        )
        run = jax.shard_map(
            one, mesh=mesh, in_specs=in_specs, out_specs=out_specs, check_vma=False
        )
        return run(*args)

    return whole
```

```python
import functools
import math

import jax
import jax.numpy as jnp
from jax import lax
from jax.experimental import pallas as pl
from jax.experimental.pallas import tpu as pltpu
from jax.sharding import PartitionSpec as P

DH = 128
LANES = 128
F32 = jnp.float32
BF16 = jnp.bfloat16
VMEM = pl.BlockSpec(memory_space=pltpu.VMEM)
SMEM = pl.BlockSpec(memory_space=pltpu.SMEM)
WINDOW = 4
PARAMS = pltpu.CompilerParams(vmem_limit_bytes=16 * 2**20)


def normalize(values):
    centre = jnp.mean(values, axis=-1, keepdims=True)
    spread = jnp.mean(jnp.square(values - centre), axis=-1, keepdims=True)
    return (values - centre) * lax.rsqrt(spread + 1e-05)


def after(value, *done):
    return lax.optimization_barrier((value, *done))[0]


def cost(flops, size):
    return pl.CostEstimate(flops=flops, bytes_accessed=size, transcendentals=0)


def ring_place(index, n):
    return index // 2 if index % 2 == 0 else n - 1 - index // 2


def owners(distances):
    n = len(distances)
    me = lax.axis_index("fsdp")
    half = lax.shift_right_logical(me, 1)
    place = jnp.where((me & 1) == 0, half, n - 1 - half)
    found = []
    for distance in distances:
        at = lax.rem(place + (distance + n), n)
        found.append(jnp.where(at < n // 2, 2 * at, 2 * (n - at) - 1))
    return found


def norm_kernel(distances, tokens_ref, normed_ref, mean_ref):
    values = tokens_ref[...].astype(F32)
    width = values.shape[1]
    centre = jnp.mean(values, axis=1, keepdims=True)
    spread = jnp.mean(jnp.square(values - centre), axis=1, keepdims=True)
    scale = lax.rsqrt(spread + 1e-05)
    mean = jnp.mean(values, axis=0, keepdims=True)
    columns = mean_ref.shape[1]
    for i in range(mean_ref.shape[0]):
        mean_ref[i : i + 1, :] = mean[:, i * columns : (i + 1) * columns]
    block = width // len(distances)
    for i, owner in enumerate(owners(distances)):
        at = pl.multiple_of(owner * block, LANES)
        piece = tokens_ref[:, pl.ds(at, block)].astype(F32)
        normed_ref[:, i * block : (i + 1) * block] = ((piece - centre) * scale).astype(BF16)


def norm_call(distances, tokens, columns):
    rows, width = tokens.shape
    return pl.pallas_call(
        functools.partial(norm_kernel, distances),
        out_shape=(
            jax.ShapeDtypeStruct((rows, width), BF16),
            jax.ShapeDtypeStruct((width // columns, columns), F32),
        ),
        in_specs=[VMEM],
        out_specs=(VMEM, VMEM),
        compiler_params=PARAMS,
        cost_estimate=cost(8 * rows * width, 4 * rows * width),
        name="norm",
    )(tokens)


def fetch(sources, buffers, sems):
    copies = [
        pltpu.make_async_copy(source, buffer, sems.at[i])
        for i, (source, buffer) in enumerate(zip(sources, buffers))
    ]
    for copy in copies:
        copy.start()

    def get(i):
        copies[i].wait()
        return buffers[i][...]

    return get


def frames_of(refs):
    return [(ref, frame) for ref in refs for frame in range(ref.shape[0])]


def times_rows(sources, first, blocks, total):
    at = first
    for block in blocks:
        depth = block.shape[0]
        rows = [ref[frame, :, at : at + depth] for ref, frame in frames_of(sources)]
        term = jnp.dot(jnp.concatenate(rows, axis=0), block, preferred_element_type=F32)
        total = term if total is None else total + term
        at += depth
    return total


def early_kernel(tensors, own_ref, core_ref, *refs):
    count = (len(refs) - 2) // 2
    sources, out_ref = refs[:count], refs[count]
    buffers, sems = refs[count + 1 : -1], refs[-1]
    get = fetch(sources, buffers, sems)
    for tensor in range(tensors):
        blocks = [get(i) for i in range(tensor, count, tensors)]
        out_ref[tensor] = times_rows((own_ref, core_ref), 0, blocks, None)


ANY = pl.BlockSpec(memory_space=pltpu.HBM)


def scratch_for(blocks):
    return [pltpu.VMEM(b.shape, b.dtype) for b in blocks] + [pltpu.SemaphoreType.DMA((len(blocks),))]


def early_call(tokens, blocks, tensors):
    rows = 2 * tokens[0].shape[0] * tokens[0].shape[1]
    columns = blocks[0].shape[1]
    depth = sum(b.shape[0] for b in blocks)
    return pl.pallas_call(
        functools.partial(early_kernel, tensors),
        out_shape=jax.ShapeDtypeStruct((tensors, rows, columns), F32),
        in_specs=[VMEM] * 2 + [ANY] * len(blocks),
        out_specs=VMEM,
        scratch_shapes=scratch_for(blocks),
        compiler_params=PARAMS,
        cost_estimate=cost(2 * rows * columns * depth, 2 * columns * depth),
        name="early",
    )(*tokens, *blocks)


def late_kernel(counts, first, own_ref, core_ref, part_ref, *refs):
    count = sum(counts)
    sources, outs = refs[:count], refs[count : count + len(counts)]
    buffers, sems = refs[count + len(counts) : -1], refs[-1]
    get = fetch(sources, buffers, sems)
    at = 0
    for tensor, number in enumerate(counts):
        blocks = [get(at + i) for i in range(number)]
        at += number
        total = times_rows((own_ref, core_ref), first, blocks, part_ref[tensor])
        outs[tensor][...] = total.astype(BF16)


def late_call(tokens, part, blocks):
    flat = [b for tensor in blocks for b in tensor]
    rows, columns = part.shape[1], part.shape[2]
    depth = sum(b.shape[0] for b in flat)
    first = tokens[0].shape[2] - sum(b.shape[0] for b in blocks[0])
    shape = jax.ShapeDtypeStruct((rows, columns), BF16)
    return pl.pallas_call(
        functools.partial(late_kernel, [len(b) for b in blocks], first),
        out_shape=[shape] * len(blocks),
        in_specs=[VMEM] * 3 + [ANY] * len(flat),
        out_specs=[VMEM] * len(blocks),
        scratch_shapes=scratch_for(flat),
        compiler_params=PARAMS,
        cost_estimate=cost(2 * rows * columns * depth, 2 * columns * depth),
        name="late",
    )(*tokens, part, *flat)


def attend_kernel(first, slots, valid_ref, mean_ref, own_ref, core_ref, part_ref, q_ref, k_ref, *refs):
    count = (len(refs) - 3) // 2
    mixed_ref, means_ref = refs[count : count + 2]
    get = fetch(refs[:count], refs[count + 2 : -1], refs[-1])
    scale = 1.0 / math.sqrt(DH)
    rows = own_ref.shape[1]
    frames = mixed_ref.shape[0] // rows
    means_ref[0, frames:, :] = mean_ref[...]
    me = lax.axis_index("seq")
    flags = [valid_ref[me ^ slot].astype(F32) for slot in slots]
    mask = jnp.concatenate([jnp.full((1, rows), flag, F32) for flag in flags], axis=1)
    blocks = [get(i) for i in range(count)]
    v = times_rows((own_ref, core_ref), first, blocks, part_ref[part_ref.shape[0] - 1]).astype(BF16)
    for head in range(v.shape[1] // DH):
        at = slice(head * DH, (head + 1) * DH)
        scores = lax.dot_general(
            q_ref[:, at], k_ref[:, at], (((1,), (1,)), ((), ())), preferred_element_type=F32
        )
        weights = jnp.exp(scores * scale) * mask
        totals = jnp.sum(weights, axis=1, keepdims=True)
        mixed = jnp.dot(weights.astype(BF16), v[:, at], preferred_element_type=F32)
        mixed = (mixed / totals).astype(BF16)
        mixed_ref[:, at] = mixed
        for frame in range(frames):
            part = mixed[frame * rows : (frame + 1) * rows].astype(F32)
            means_ref[0, frame : frame + 1, at] = jnp.mean(part, axis=0, keepdims=True)


def attend_call(slots, valid, token_mean, tokens, part, q, k, blocks):
    rows, columns = q.shape
    depth = tokens[0].shape[2]
    means = rows // tokens[0].shape[1] + token_mean.shape[0]
    first = depth - sum(b.shape[0] for b in blocks)
    return pl.pallas_call(
        functools.partial(attend_kernel, first, slots),
        out_shape=(
            jax.ShapeDtypeStruct((rows, columns), BF16),
            jax.ShapeDtypeStruct((1, means, columns), F32),
        ),
        in_specs=[SMEM] + [VMEM] * 6 + [ANY] * len(blocks),
        out_specs=(VMEM, VMEM),
        scratch_shapes=scratch_for(blocks),
        compiler_params=PARAMS,
        cost_estimate=cost(2 * rows * columns * (depth + 2 * rows), 2 * columns * depth),
        name="attend",
    )(valid, token_mean, *tokens, part, q, k, *blocks)


def times_block(values, parts):
    total, at = None, 0
    for part in parts:
        term = jnp.dot(values[:, at : at + part.shape[0]], part[...], preferred_element_type=F32)
        total = term if total is None else total + term
        at += part.shape[0]
    return total


def out_kernel(counts, mixed_ref, *refs):
    blocks, at = [], 0
    for count in counts:
        blocks.append(refs[at : at + count])
        at += count
    send_ref, keep_ref = refs[at:]
    half = mixed_ref.shape[0] // 2
    columns = blocks[0][0].shape[1]
    for i, parts in enumerate(blocks):
        result = times_block(mixed_ref, parts)
        keep_ref[:, i * columns : (i + 1) * columns] = result[:half]
        send_ref[:, i * columns : (i + 1) * columns] = result[half:].astype(BF16)


def out_call(mixed, blocks):
    flat = [part for parts in blocks for part in parts]
    rows, depth = mixed.shape
    columns = len(blocks) * blocks[0][0].shape[1]
    return pl.pallas_call(
        functools.partial(out_kernel, [len(parts) for parts in blocks]),
        out_shape=(
            jax.ShapeDtypeStruct((rows // 2, columns), BF16),
            jax.ShapeDtypeStruct((rows // 2, columns), F32),
        ),
        in_specs=[VMEM] * (1 + len(flat)),
        out_specs=(VMEM, VMEM),
        compiler_params=PARAMS,
        cost_estimate=cost(2 * rows * columns * depth, 2 * depth * columns + 6 * rows * columns),
        name="out",
    )(mixed, *flat)


def pool_kernel(counts, frames, means_ref, *refs):
    blocks, at = [], 0
    for count in counts:
        blocks.append(refs[at : at + count])
        at += count
    send_ref, keep_ref, held = refs[at:]
    windows = means_ref.shape[0]
    rows = windows * frames
    for r in range(windows):
        for frame in range(frames):
            to = frame * windows + r
            held[to : to + 1, :] = means_ref[r, frame : frame + 1, :]
    values = held[...]
    upper = values.astype(BF16)
    lower = (values - upper.astype(F32)).astype(BF16)
    both = jnp.concatenate([upper, lower], axis=0)
    columns = blocks[0][0].shape[1]
    for i, parts in enumerate(blocks):
        result = times_block(both, parts)
        result = result[:rows] + result[rows:]
        keep_ref[:, i * columns : (i + 1) * columns] = result[: rows // 2]
        send_ref[:, i * columns : (i + 1) * columns] = result[rows // 2 :]


def pool_call(means, blocks, frames):
    flat = [part for parts in blocks for part in parts]
    rows, depth = frames * means.shape[0], means.shape[2]
    columns = len(blocks) * blocks[0][0].shape[1]
    shape = jax.ShapeDtypeStruct((rows // 2, columns), F32)
    return pl.pallas_call(
        functools.partial(pool_kernel, [len(parts) for parts in blocks], frames),
        out_shape=(shape, shape),
        in_specs=[VMEM] * (1 + len(flat)),
        out_specs=(VMEM, VMEM),
        scratch_shapes=[pltpu.VMEM((rows, depth), F32)],
        compiler_params=PARAMS,
        cost_estimate=cost(4 * rows * columns * depth, 2 * depth * columns),
        name="pool",
    )(means, *flat)


def finish_kernel(distances, groups, tokens_ref, *refs):
    out_ref = refs[-1]
    rows = tokens_ref.shape[0]
    slot = 0
    block = tokens_ref.shape[1] // len(distances)
    found = owners(distances)
    for g in range(groups):
        sums, came = refs[2 * g], refs[2 * g + 1]
        for i in range(sums.shape[1] // block):
            at = pl.ds(pl.multiple_of(found[slot] * block, LANES), block)
            here = slice(i * block, (i + 1) * block)
            total = sums[:rows, here] + came[:, here].astype(F32)
            out_ref[:, at] = (tokens_ref[:, at].astype(F32) + total).astype(BF16)
            slot += 1


def finish_call(distances, tokens, sums):
    flat = [part for pair in sums for part in pair]
    return pl.pallas_call(
        functools.partial(finish_kernel, distances, len(sums)),
        out_shape=jax.ShapeDtypeStruct(tokens.shape, BF16),
        in_specs=[VMEM] * (1 + len(flat)),
        out_specs=VMEM,
        compiler_params=PARAMS,
        cost_estimate=cost(4 * tokens.size, 10 * tokens.size),
        name="finish",
    )(tokens, *flat)


def head_kernel(distances, slots, sums_ref, came_ref, means_ref, act_ref, bias_ref, out_ref, pooled):
    windows, width = pooled.shape
    columns = means_ref.shape[2]
    first = means_ref.shape[1] - width // columns
    for i in range(width // columns):
        pooled[:, i * columns : (i + 1) * columns] = means_ref[:, first + i, :]
    block = width // len(distances)
    for i, owner in enumerate(owners(distances)):
        at = pl.ds(pl.multiple_of(owner * block, LANES), block)
        here = slice(i * block, (i + 1) * block)
        pooled[:, at] += sums_ref[:windows, here] + came_ref[:, here]
    values = normalize(pooled[...]).astype(BF16)
    logits = jnp.dot(values, act_ref[...], preferred_element_type=F32) + bias_ref[...]
    me = lax.axis_index("fsdp")
    for i, slot in enumerate(slots):
        out_ref[pl.ds(me ^ slot, 1), 0, 0, :] = logits[i : i + 1]


def head_call(distances, slots, sums, came, means, act, bias):
    width, columns = act.shape
    return pl.pallas_call(
        functools.partial(head_kernel, distances, slots),
        out_shape=jax.ShapeDtypeStruct((means.shape[0], 1, 1, columns), F32),
        in_specs=[VMEM] * 5,
        out_specs=VMEM,
        scratch_shapes=[pltpu.VMEM((means.shape[0], width), F32)],
        compiler_params=PARAMS,
        cost_estimate=cost(2 * means.shape[0] * act.size, 2 * act.size),
        name="head",
    )(sums, came, means, act, bias)


def make(mesh):
    fsdp, seq = mesh.shape["fsdp"], mesh.shape["seq"]
    order = sorted(range(fsdp), key=lambda i: ring_place(i, fsdp))
    forward = [(order[i], order[(i + 1) % fsdp]) for i in range(fsdp)]
    backward = [(b, a) for a, b in forward]
    wide_bits = [1 << i for i in range(1, (seq - 1).bit_length())]
    distances = [0]
    for t in range(1, fsdp // 2):
        distances += [-t, t]
    distances.append(fsdp // 2)

    def over_fsdp(value, bit):
        return lax.ppermute(value, "fsdp", [(i, i ^ bit) for i in range(fsdp)])

    def over_seq(value, bit):
        return lax.ppermute(value, "seq", [(i, i ^ bit) for i in range(seq)])

    def per_device(tokens, frame_valid, w_qkv, w_out, w_act, class_table, cam_bias):
        frame_rows, width = tokens.shape[3], tokens.shape[4]
        own_tokens = tokens.reshape(frame_rows, width)
        by_tensor = jnp.transpose(w_qkv, (1, 0, 2))
        sent = []
        chains = {"q": by_tensor[0], "k": by_tensor[1], "v": by_tensor[2], "o": w_out}
        edge = {name: [start, start] for name, start in chains.items()}
        came = {name: [start] for name, start in chains.items()}

        def move(name, way):
            value = edge[name][way]
            if len(sent) >= WINDOW:
                value = after(value, sent[-WINDOW])
            value = lax.ppermute(value, "fsdp", backward if way else forward)
            edge[name][way] = value
            came[name].append(value)
            sent.append(value)

        def both(name):
            move(name, 0)
            move(name, 1)

        normed, token_mean = norm_call(distances, own_tokens, w_qkv.shape[2])
        own = normed[None]
        frame_slots = [0]
        for bit in wide_bits:
            own = jnp.concatenate([own, over_seq(own, bit)], axis=0)
            frame_slots = frame_slots + [o ^ bit for o in frame_slots]
        frame_slots = frame_slots + [o ^ 1 for o in frame_slots]

        steps = fsdp // 2
        soon = 2 if steps > 2 else 1
        for _ in range(soon):
            for name in "qkv":
                both(name)
        count = 2 * soon + 1
        rows = (own, over_seq(own, 1))
        part = early_call(rows, [came[name][i] for i in range(count) for name in "qkv"], 3)
        for _ in range(soon, steps - 1):
            for name in "qkv":
                both(name)
        both("o")
        move("q", 0)
        move("k", 1)
        move("v", 0)
        for _ in range(1, steps - 1):
            both("o")
        move("o", 1)

        qkv, blocks = [came[name] for name in "qkv"], [[block] for block in came["o"]]

        q, k = late_call(rows, part, [qkv[0][count:], qkv[1][count:]])
        mixed, means = attend_call(
            frame_slots, frame_valid.reshape(seq), token_mean, rows, part, q, k, qkv[2][count:]
        )

        def reduce_once(keep, arrived, to):
            total = keep + arrived.astype(F32)
            half = total.shape[0] // 2
            return total[:half], total[half:].astype(to)

        def reduce_all(send, keep, to, *done):
            crossed = arrived = over_seq(send, 1)
            for bit in wide_bits[::-1]:
                keep, leave = reduce_once(keep, arrived, to)
                arrived = over_seq(after(leave, *done) if done else leave, bit)
            return keep, arrived, crossed

        windows = [0]
        bits = [1 << i for i in range((fsdp - 1).bit_length())][::-1]
        seen = []

        def gather(means, bit, *done):
            seen.append(over_fsdp(after(means, *done) if done else means, bit))
            windows.extend([window ^ bit for window in windows])
            return jnp.concatenate([means, seen[-1]], axis=0)

        means = gather(means, bits[0])
        cut = min(5, len(blocks) - 1)
        near, last = [block for (block,) in blocks[cut:-1]], blocks[-1][0]
        *early, crossed = reduce_all(*out_call(after(mixed, seen[0]), blocks[:cut]), BF16)
        waits = {2: (early[1],)}
        for i, bit in enumerate(bits[1:], 1):
            means = gather(means, bit, *waits.get(i, ()))

        pool_keep, pool_came, _ = reduce_all(*pool_call(after(means, early[1]), blocks, seq), F32)
        later = reduce_all(*out_call(after(mixed, means), blocks[cut:]), BF16)
        sums = [early, later[:2]]
        hidden = finish_call(distances, own_tokens, sums)

        camera_ids = jnp.arange(cam_bias.shape[0], dtype=jnp.int32)
        onehot = (class_table[:, None] == camera_ids[None, :]).astype(F32)
        bias = jnp.dot(onehot, cam_bias, precision=lax.Precision.HIGHEST)[None]
        logits = head_call(distances, windows, pool_keep, pool_came, means, w_act, bias)
        return hidden.reshape(tokens.shape), logits

    return per_device


def plain(tokens, frame_valid, w_qkv, w_out, w_act, class_table, cam_bias):
    windows_here, frame_rows, width = tokens.shape[0], tokens.shape[3], tokens.shape[4]
    own_rows = tokens[:, 0, 0].astype(F32)
    normed = normalize(own_rows).astype(BF16)
    gathered = lax.all_gather(normed[:, None], "seq", axis=1, tiled=True)
    frame_count = gathered.shape[1]
    span = frame_count * frame_rows
    rows = gathered.reshape(windows_here, span, width)
    full_qkv = lax.all_gather(w_qkv, "fsdp", axis=0, tiled=True)
    projected = jnp.einsum("wsd,dcn->wscn", rows, full_qkv, preferred_element_type=F32)
    heads = full_qkv.shape[2] // DH
    projected = projected.astype(BF16).reshape(windows_here, span, 3, heads, DH)
    q, k, v = projected[:, :, 0], projected[:, :, 1], projected[:, :, 2]
    key_mask = jnp.repeat(frame_valid[:, 0].astype(F32), frame_rows, axis=1)
    scores = jnp.einsum("wqhe,wkhe->whqk", q, k, preferred_element_type=F32) / math.sqrt(DH)
    weights = jnp.exp(scores) * key_mask[:, None, None, :]
    totals = jnp.sum(weights, axis=-1)
    mixed = jnp.einsum("whqk,wkhe->wqhe", weights.astype(BF16), v, preferred_element_type=F32)
    mixed = (mixed / jnp.transpose(totals, (0, 2, 1))[:, :, :, None]).astype(BF16)
    mixed = mixed.reshape(windows_here, frame_count, frame_rows, heads * DH)
    mixed = jnp.transpose(mixed, (1, 0, 2, 3)).reshape(-1, heads * DH)
    full_out = lax.all_gather(w_out, "fsdp", axis=1, tiled=True)
    branch = lax.psum_scatter(
        jnp.dot(mixed, full_out, preferred_element_type=F32), "seq", scatter_dimension=0, tiled=True
    )
    hidden = (own_rows + branch.reshape(windows_here, frame_rows, width)).astype(BF16)
    wide = lax.optimization_barrier(hidden).astype(F32)
    pooled = normalize(jnp.mean(wide, axis=1)).astype(BF16)
    camera_ids = jnp.arange(cam_bias.shape[0], dtype=jnp.int32)
    onehot = (class_table[:, None] == camera_ids[None, :]).astype(F32)
    bias = jnp.dot(onehot, cam_bias, precision=lax.Precision.HIGHEST)
    everywhere = lax.all_gather(pooled, "fsdp", axis=0, tiled=True)
    logits = jnp.dot(everywhere, w_act, preferred_element_type=F32) + bias[None, :]
    return (
        hidden.reshape(windows_here, 1, 1, frame_rows, width),
        logits.reshape(logits.shape[0], 1, 1, logits.shape[1]),
    )


def solution(mesh):
    fsdp, seq = mesh.shape["fsdp"], mesh.shape["seq"]

    def whole(tokens, frame_valid, w_qkv, w_out, w_act, class_table, cam_bias):
        args = (tokens, frame_valid, w_qkv, w_out, w_act, class_table, cam_bias)
        powers = all(n & (n - 1) == 0 for n in (fsdp, seq)) and fsdp >= 4 and seq >= 2
        aligned = w_qkv.shape[0] % (fsdp * LANES) == 0 and w_qkv.shape[2] % (seq * 2 * DH) == 0
        one_window = tokens.shape[0] == mesh.shape["groups"] * fsdp
        one_window = one_window and tokens.shape[1] == mesh.shape["sub"] and tokens.shape[2] == seq
        one = make(mesh) if powers and aligned and one_window else plain
        in_specs = (
            P(("groups", "fsdp"), "sub", "seq", None, None),
            P(("groups", "fsdp"), "sub", None),
            P("fsdp", None, "seq"),
            P("seq", "fsdp"),
            P(None, "fsdp"),
            P("fsdp"),
            P(),
        )
        out_specs = (
            P(("groups", "fsdp"), "sub", "seq", None, None),
            P("groups", "sub", "seq", "fsdp"),
        )
        run = jax.shard_map(
            one, mesh=mesh, in_specs=in_specs, out_specs=out_specs, check_vma=False
        )
        return run(*args)

    return whole
```

```python
import functools
import math

import jax
import jax.numpy as jnp
from jax import lax
from jax.experimental import pallas as pl
from jax.experimental.pallas import tpu as pltpu
from jax.sharding import PartitionSpec as P

DH = 128
LANES = 128
F32 = jnp.float32
BF16 = jnp.bfloat16
VMEM = pl.BlockSpec(memory_space=pltpu.VMEM)
SMEM = pl.BlockSpec(memory_space=pltpu.SMEM)
WINDOW = 4
PARAMS = pltpu.CompilerParams(vmem_limit_bytes=16 * 2**20)


def normalize(values):
    centre = jnp.mean(values, axis=-1, keepdims=True)
    spread = jnp.mean(jnp.square(values - centre), axis=-1, keepdims=True)
    return (values - centre) * lax.rsqrt(spread + 1e-05)


def after(value, *done):
    return lax.optimization_barrier((value, *done))[0]


def cost(flops, size):
    return pl.CostEstimate(flops=flops, bytes_accessed=size, transcendentals=0)


def ring_place(index, n):
    return index // 2 if index % 2 == 0 else n - 1 - index // 2


def owners(distances):
    n = len(distances)
    me = lax.axis_index("fsdp")
    half = lax.shift_right_logical(me, 1)
    place = jnp.where((me & 1) == 0, half, n - 1 - half)
    found = []
    for distance in distances:
        at = lax.rem(place + (distance + n), n)
        found.append(jnp.where(at < n // 2, 2 * at, 2 * (n - at) - 1))
    return found


def norm_kernel(distances, tokens_ref, normed_ref, mean_ref):
    values = tokens_ref[...].astype(F32)
    width = values.shape[1]
    centre = jnp.mean(values, axis=1, keepdims=True)
    spread = jnp.mean(jnp.square(values - centre), axis=1, keepdims=True)
    scale = lax.rsqrt(spread + 1e-05)
    mean = jnp.mean(values, axis=0, keepdims=True)
    columns = mean_ref.shape[1]
    for i in range(mean_ref.shape[0]):
        mean_ref[i : i + 1, :] = mean[:, i * columns : (i + 1) * columns]
    block = width // len(distances)
    for i, owner in enumerate(owners(distances)):
        at = pl.multiple_of(owner * block, LANES)
        piece = tokens_ref[:, pl.ds(at, block)].astype(F32)
        normed_ref[:, i * block : (i + 1) * block] = ((piece - centre) * scale).astype(BF16)


def norm_call(distances, tokens, columns):
    rows, width = tokens.shape
    return pl.pallas_call(
        functools.partial(norm_kernel, distances),
        out_shape=(
            jax.ShapeDtypeStruct((rows, width), BF16),
            jax.ShapeDtypeStruct((width // columns, columns), F32),
        ),
        in_specs=[VMEM],
        out_specs=(VMEM, VMEM),
        compiler_params=PARAMS,
        cost_estimate=cost(8 * rows * width, 4 * rows * width),
        name="norm",
    )(tokens)


def fetch(sources, buffers, sems):
    copies = [
        pltpu.make_async_copy(source, buffer, sems.at[i])
        for i, (source, buffer) in enumerate(zip(sources, buffers))
    ]
    for copy in copies:
        copy.start()

    def get(i):
        copies[i].wait()
        return buffers[i][...]

    return get


def frames_of(refs):
    return [(ref, frame) for ref in refs for frame in range(ref.shape[0])]


def times_rows(sources, first, blocks, total):
    at = first
    for block in blocks:
        depth = block.shape[0]
        rows = [ref[frame, :, at : at + depth] for ref, frame in frames_of(sources)]
        term = jnp.dot(jnp.concatenate(rows, axis=0), block, preferred_element_type=F32)
        total = term if total is None else total + term
        at += depth
    return total


def early_kernel(tensors, own_ref, core_ref, *refs):
    count = (len(refs) - 2) // 2
    sources, out_ref = refs[:count], refs[count]
    buffers, sems = refs[count + 1 : -1], refs[-1]
    get = fetch(sources, buffers, sems)
    for tensor in range(tensors):
        blocks = [get(i) for i in range(tensor, count, tensors)]
        out_ref[tensor] = times_rows((own_ref, core_ref), 0, blocks, None)


ANY = pl.BlockSpec(memory_space=pltpu.HBM)


def scratch_for(blocks):
    return [pltpu.VMEM(b.shape, b.dtype) for b in blocks] + [pltpu.SemaphoreType.DMA((len(blocks),))]


def early_call(tokens, blocks, tensors):
    rows = 2 * tokens[0].shape[0] * tokens[0].shape[1]
    columns = blocks[0].shape[1]
    depth = sum(b.shape[0] for b in blocks)
    return pl.pallas_call(
        functools.partial(early_kernel, tensors),
        out_shape=jax.ShapeDtypeStruct((tensors, rows, columns), F32),
        in_specs=[VMEM] * 2 + [ANY] * len(blocks),
        out_specs=VMEM,
        scratch_shapes=scratch_for(blocks),
        compiler_params=PARAMS,
        cost_estimate=cost(2 * rows * columns * depth, 2 * columns * depth),
        name="early",
    )(*tokens, *blocks)


def late_kernel(counts, first, own_ref, core_ref, part_ref, *refs):
    count = sum(counts)
    sources, outs = refs[:count], refs[count : count + len(counts)]
    buffers, sems = refs[count + len(counts) : -1], refs[-1]
    get = fetch(sources, buffers, sems)
    at = 0
    for tensor, number in enumerate(counts):
        blocks = [get(at + i) for i in range(number)]
        at += number
        total = times_rows((own_ref, core_ref), first, blocks, part_ref[tensor])
        outs[tensor][...] = total.astype(BF16)


def late_call(tokens, part, blocks):
    flat = [b for tensor in blocks for b in tensor]
    rows, columns = part.shape[1], part.shape[2]
    depth = sum(b.shape[0] for b in flat)
    first = tokens[0].shape[2] - sum(b.shape[0] for b in blocks[0])
    shape = jax.ShapeDtypeStruct((rows, columns), BF16)
    return pl.pallas_call(
        functools.partial(late_kernel, [len(b) for b in blocks], first),
        out_shape=[shape] * len(blocks),
        in_specs=[VMEM] * 3 + [ANY] * len(flat),
        out_specs=[VMEM] * len(blocks),
        scratch_shapes=scratch_for(flat),
        compiler_params=PARAMS,
        cost_estimate=cost(2 * rows * columns * depth, 2 * columns * depth),
        name="late",
    )(*tokens, part, *flat)


def attend_kernel(first, slots, valid_ref, mean_ref, own_ref, core_ref, part_ref, q_ref, k_ref, *refs):
    count = (len(refs) - 3) // 2
    mixed_ref, means_ref = refs[count : count + 2]
    get = fetch(refs[:count], refs[count + 2 : -1], refs[-1])
    scale = 1.0 / math.sqrt(DH)
    rows = own_ref.shape[1]
    frames = mixed_ref.shape[0] // rows
    means_ref[0, frames:, :] = mean_ref[...]
    me = lax.axis_index("seq")
    flags = [valid_ref[me ^ slot].astype(F32) for slot in slots]
    mask = jnp.concatenate([jnp.full((1, rows), flag, F32) for flag in flags], axis=1)
    blocks = [get(i) for i in range(count)]
    v = times_rows((own_ref, core_ref), first, blocks, part_ref[part_ref.shape[0] - 1]).astype(BF16)
    for head in range(v.shape[1] // DH):
        at = slice(head * DH, (head + 1) * DH)
        scores = lax.dot_general(
            q_ref[:, at], k_ref[:, at], (((1,), (1,)), ((), ())), preferred_element_type=F32
        )
        weights = jnp.exp(scores * scale) * mask
        totals = jnp.sum(weights, axis=1, keepdims=True)
        mixed = jnp.dot(weights.astype(BF16), v[:, at], preferred_element_type=F32)
        mixed = (mixed / totals).astype(BF16)
        mixed_ref[:, at] = mixed
        for frame in range(frames):
            part = mixed[frame * rows : (frame + 1) * rows].astype(F32)
            means_ref[0, frame : frame + 1, at] = jnp.mean(part, axis=0, keepdims=True)


def attend_call(slots, valid, token_mean, tokens, part, q, k, blocks):
    rows, columns = q.shape
    depth = tokens[0].shape[2]
    means = rows // tokens[0].shape[1] + token_mean.shape[0]
    first = depth - sum(b.shape[0] for b in blocks)
    return pl.pallas_call(
        functools.partial(attend_kernel, first, slots),
        out_shape=(
            jax.ShapeDtypeStruct((rows, columns), BF16),
            jax.ShapeDtypeStruct((1, means, columns), F32),
        ),
        in_specs=[SMEM] + [VMEM] * 6 + [ANY] * len(blocks),
        out_specs=(VMEM, VMEM),
        scratch_shapes=scratch_for(blocks),
        compiler_params=PARAMS,
        cost_estimate=cost(2 * rows * columns * (depth + 2 * rows), 2 * columns * depth),
        name="attend",
    )(valid, token_mean, *tokens, part, q, k, *blocks)


def times_block(values, parts):
    total, at = None, 0
    for part in parts:
        term = jnp.dot(values[:, at : at + part.shape[0]], part[...], preferred_element_type=F32)
        total = term if total is None else total + term
        at += part.shape[0]
    return total


def out_kernel(counts, mixed_ref, *refs):
    blocks, at = [], 0
    for count in counts:
        blocks.append(refs[at : at + count])
        at += count
    send_ref, keep_ref = refs[at:]
    half = mixed_ref.shape[0] // 2
    columns = blocks[0][0].shape[1]
    for i, parts in enumerate(blocks):
        result = times_block(mixed_ref, parts)
        keep_ref[:, i * columns : (i + 1) * columns] = result[:half]
        send_ref[:, i * columns : (i + 1) * columns] = result[half:].astype(BF16)


def out_call(mixed, blocks):
    flat = [part for parts in blocks for part in parts]
    rows, depth = mixed.shape
    columns = len(blocks) * blocks[0][0].shape[1]
    return pl.pallas_call(
        functools.partial(out_kernel, [len(parts) for parts in blocks]),
        out_shape=(
            jax.ShapeDtypeStruct((rows // 2, columns), BF16),
            jax.ShapeDtypeStruct((rows // 2, columns), F32),
        ),
        in_specs=[VMEM] * (1 + len(flat)),
        out_specs=(VMEM, VMEM),
        compiler_params=PARAMS,
        cost_estimate=cost(2 * rows * columns * depth, 2 * depth * columns + 6 * rows * columns),
        name="out",
    )(mixed, *flat)


def pool_kernel(counts, frames, means_ref, *refs):
    blocks, at = [], 0
    for count in counts:
        blocks.append(refs[at : at + count])
        at += count
    send_ref, keep_ref, held = refs[at:]
    windows = means_ref.shape[0]
    rows = windows * frames
    for r in range(windows):
        for frame in range(frames):
            to = frame * windows + r
            held[to : to + 1, :] = means_ref[r, frame : frame + 1, :]
    values = held[...]
    upper = values.astype(BF16)
    lower = (values - upper.astype(F32)).astype(BF16)
    both = jnp.concatenate([upper, lower], axis=0)
    columns = blocks[0][0].shape[1]
    for i, parts in enumerate(blocks):
        result = times_block(both, parts)
        result = result[:rows] + result[rows:]
        keep_ref[:, i * columns : (i + 1) * columns] = result[: rows // 2]
        send_ref[:, i * columns : (i + 1) * columns] = result[rows // 2 :]


def pool_call(means, blocks, frames):
    flat = [part for parts in blocks for part in parts]
    rows, depth = frames * means.shape[0], means.shape[2]
    columns = len(blocks) * blocks[0][0].shape[1]
    shape = jax.ShapeDtypeStruct((rows // 2, columns), F32)
    return pl.pallas_call(
        functools.partial(pool_kernel, [len(parts) for parts in blocks], frames),
        out_shape=(shape, shape),
        in_specs=[VMEM] * (1 + len(flat)),
        out_specs=(VMEM, VMEM),
        scratch_shapes=[pltpu.VMEM((rows, depth), F32)],
        compiler_params=PARAMS,
        cost_estimate=cost(4 * rows * columns * depth, 2 * depth * columns),
        name="pool",
    )(means, *flat)


def finish_kernel(distances, groups, tokens_ref, *refs):
    out_ref = refs[-1]
    rows = tokens_ref.shape[0]
    slot = 0
    block = tokens_ref.shape[1] // len(distances)
    found = owners(distances)
    for g in range(groups):
        sums, came = refs[2 * g], refs[2 * g + 1]
        for i in range(sums.shape[1] // block):
            at = pl.ds(pl.multiple_of(found[slot] * block, LANES), block)
            here = slice(i * block, (i + 1) * block)
            total = sums[:rows, here] + came[:, here].astype(F32)
            out_ref[:, at] = (tokens_ref[:, at].astype(F32) + total).astype(BF16)
            slot += 1


def finish_call(distances, tokens, sums):
    flat = [part for pair in sums for part in pair]
    return pl.pallas_call(
        functools.partial(finish_kernel, distances, len(sums)),
        out_shape=jax.ShapeDtypeStruct(tokens.shape, BF16),
        in_specs=[VMEM] * (1 + len(flat)),
        out_specs=VMEM,
        compiler_params=PARAMS,
        cost_estimate=cost(4 * tokens.size, 10 * tokens.size),
        name="finish",
    )(tokens, *flat)


def head_kernel(distances, slots, sums_ref, came_ref, means_ref, act_ref, bias_ref, out_ref, pooled):
    windows, width = pooled.shape
    columns = means_ref.shape[2]
    first = means_ref.shape[1] - width // columns
    for i in range(width // columns):
        pooled[:, i * columns : (i + 1) * columns] = means_ref[:, first + i, :]
    block = width // len(distances)
    for i, owner in enumerate(owners(distances)):
        at = pl.ds(pl.multiple_of(owner * block, LANES), block)
        here = slice(i * block, (i + 1) * block)
        pooled[:, at] += sums_ref[:windows, here] + came_ref[:, here]
    values = normalize(pooled[...]).astype(BF16)
    logits = jnp.dot(values, act_ref[...], preferred_element_type=F32) + bias_ref[...]
    me = lax.axis_index("fsdp")
    for i, slot in enumerate(slots):
        out_ref[pl.ds(me ^ slot, 1), 0, 0, :] = logits[i : i + 1]


def head_call(distances, slots, sums, came, means, act, bias):
    width, columns = act.shape
    return pl.pallas_call(
        functools.partial(head_kernel, distances, slots),
        out_shape=jax.ShapeDtypeStruct((means.shape[0], 1, 1, columns), F32),
        in_specs=[VMEM] * 5,
        out_specs=VMEM,
        scratch_shapes=[pltpu.VMEM((means.shape[0], width), F32)],
        compiler_params=PARAMS,
        cost_estimate=cost(2 * means.shape[0] * act.size, 2 * act.size),
        name="head",
    )(sums, came, means, act, bias)


def make(mesh):
    fsdp, seq = mesh.shape["fsdp"], mesh.shape["seq"]
    order = sorted(range(fsdp), key=lambda i: ring_place(i, fsdp))
    forward = [(order[i], order[(i + 1) % fsdp]) for i in range(fsdp)]
    backward = [(b, a) for a, b in forward]
    wide_bits = [1 << i for i in range(1, (seq - 1).bit_length())]
    distances = [0]
    for t in range(1, fsdp // 2):
        distances += [-t, t]
    distances.append(fsdp // 2)

    def over_fsdp(value, bit):
        return lax.ppermute(value, "fsdp", [(i, i ^ bit) for i in range(fsdp)])

    def over_seq(value, bit):
        return lax.ppermute(value, "seq", [(i, i ^ bit) for i in range(seq)])

    def per_device(tokens, frame_valid, w_qkv, w_out, w_act, class_table, cam_bias):
        frame_rows, width = tokens.shape[3], tokens.shape[4]
        own_tokens = tokens.reshape(frame_rows, width)
        by_tensor = jnp.transpose(w_qkv, (1, 0, 2))
        sent = []
        chains = {"q": by_tensor[0], "k": by_tensor[1], "v": by_tensor[2], "o": w_out}
        edge = {name: [start, start] for name, start in chains.items()}
        came = {name: [start] for name, start in chains.items()}

        def move(name, way):
            value = edge[name][way]
            if len(sent) >= WINDOW:
                value = after(value, sent[-WINDOW])
            value = lax.ppermute(value, "fsdp", backward if way else forward)
            edge[name][way] = value
            came[name].append(value)
            sent.append(value)

        def both(name):
            move(name, 0)
            move(name, 1)

        normed, token_mean = norm_call(distances, own_tokens, w_qkv.shape[2])
        own = normed[None]
        frame_slots = [0]
        for bit in wide_bits:
            own = jnp.concatenate([own, over_seq(own, bit)], axis=0)
            frame_slots = frame_slots + [o ^ bit for o in frame_slots]
        frame_slots = frame_slots + [o ^ 1 for o in frame_slots]

        steps = fsdp // 2
        soon = 2 if steps > 2 else 1
        for _ in range(soon):
            for name in "qkv":
                both(name)
        count = 2 * soon + 1
        rows = (own, over_seq(own, 1))
        part = early_call(rows, [came[name][i] for i in range(count) for name in "qkv"], 3)
        for _ in range(soon, steps - 1):
            for name in "qkv":
                both(name)
        both("o")
        move("q", 0)
        move("k", 1)
        move("v", 0)
        for _ in range(1, steps - 1):
            move("o", 1)
            move("o", 0)
            came["o"][-2:] = came["o"][:-3:-1]
        move("o", 1)

        qkv, blocks = [came[name] for name in "qkv"], [[block] for block in came["o"]]

        q, k = late_call(rows, part, [qkv[0][count:], qkv[1][count:]])
        mixed, means = attend_call(
            frame_slots, frame_valid.reshape(seq), token_mean, rows, part, q, k, qkv[2][count:]
        )

        def reduce_once(keep, arrived, to):
            total = keep + arrived.astype(F32)
            half = total.shape[0] // 2
            return total[:half], total[half:].astype(to)

        def reduce_all(send, keep, to, *done):
            crossed = arrived = over_seq(send, 1)
            for bit in wide_bits[::-1]:
                keep, leave = reduce_once(keep, arrived, to)
                arrived = over_seq(after(leave, *done) if done else leave, bit)
            return keep, arrived, crossed

        windows = [0]
        bits = [1 << i for i in range((fsdp - 1).bit_length())][::-1]
        seen = []

        def gather(means, bit, *done):
            seen.append(over_fsdp(after(means, *done) if done else means, bit))
            windows.extend([window ^ bit for window in windows])
            return jnp.concatenate([means, seen[-1]], axis=0)

        means = gather(means, bits[0])
        cut = min(5, len(blocks) - 1)
        near, last = [block for (block,) in blocks[cut:-1]], blocks[-1][0]
        *early, crossed = reduce_all(*out_call(mixed, blocks[:cut]), BF16)
        waits = {1: (crossed,), 2: (early[1], *near)}
        for i, bit in enumerate(bits[1:], 1):
            means = gather(means, bit, *waits.get(i, ()))

        pool_keep, pool_came, _ = reduce_all(*pool_call(after(means, early[1]), blocks, seq), F32)
        later = reduce_all(*out_call(after(mixed, means), blocks[cut:]), BF16)
        sums = [early, later[:2]]
        hidden = finish_call(distances, own_tokens, sums)

        camera_ids = jnp.arange(cam_bias.shape[0], dtype=jnp.int32)
        onehot = (class_table[:, None] == camera_ids[None, :]).astype(F32)
        bias = jnp.dot(onehot, cam_bias, precision=lax.Precision.HIGHEST)[None]
        logits = head_call(distances, windows, pool_keep, pool_came, means, w_act, bias)
        return hidden.reshape(tokens.shape), logits

    return per_device


def plain(tokens, frame_valid, w_qkv, w_out, w_act, class_table, cam_bias):
    windows_here, frame_rows, width = tokens.shape[0], tokens.shape[3], tokens.shape[4]
    own_rows = tokens[:, 0, 0].astype(F32)
    normed = normalize(own_rows).astype(BF16)
    gathered = lax.all_gather(normed[:, None], "seq", axis=1, tiled=True)
    frame_count = gathered.shape[1]
    span = frame_count * frame_rows
    rows = gathered.reshape(windows_here, span, width)
    full_qkv = lax.all_gather(w_qkv, "fsdp", axis=0, tiled=True)
    projected = jnp.einsum("wsd,dcn->wscn", rows, full_qkv, preferred_element_type=F32)
    heads = full_qkv.shape[2] // DH
    projected = projected.astype(BF16).reshape(windows_here, span, 3, heads, DH)
    q, k, v = projected[:, :, 0], projected[:, :, 1], projected[:, :, 2]
    key_mask = jnp.repeat(frame_valid[:, 0].astype(F32), frame_rows, axis=1)
    scores = jnp.einsum("wqhe,wkhe->whqk", q, k, preferred_element_type=F32) / math.sqrt(DH)
    weights = jnp.exp(scores) * key_mask[:, None, None, :]
    totals = jnp.sum(weights, axis=-1)
    mixed = jnp.einsum("whqk,wkhe->wqhe", weights.astype(BF16), v, preferred_element_type=F32)
    mixed = (mixed / jnp.transpose(totals, (0, 2, 1))[:, :, :, None]).astype(BF16)
    mixed = mixed.reshape(windows_here, frame_count, frame_rows, heads * DH)
    mixed = jnp.transpose(mixed, (1, 0, 2, 3)).reshape(-1, heads * DH)
    full_out = lax.all_gather(w_out, "fsdp", axis=1, tiled=True)
    branch = lax.psum_scatter(
        jnp.dot(mixed, full_out, preferred_element_type=F32), "seq", scatter_dimension=0, tiled=True
    )
    hidden = (own_rows + branch.reshape(windows_here, frame_rows, width)).astype(BF16)
    wide = lax.optimization_barrier(hidden).astype(F32)
    pooled = normalize(jnp.mean(wide, axis=1)).astype(BF16)
    camera_ids = jnp.arange(cam_bias.shape[0], dtype=jnp.int32)
    onehot = (class_table[:, None] == camera_ids[None, :]).astype(F32)
    bias = jnp.dot(onehot, cam_bias, precision=lax.Precision.HIGHEST)
    everywhere = lax.all_gather(pooled, "fsdp", axis=0, tiled=True)
    logits = jnp.dot(everywhere, w_act, preferred_element_type=F32) + bias[None, :]
    return (
        hidden.reshape(windows_here, 1, 1, frame_rows, width),
        logits.reshape(logits.shape[0], 1, 1, logits.shape[1]),
    )


def solution(mesh):
    fsdp, seq = mesh.shape["fsdp"], mesh.shape["seq"]

    def whole(tokens, frame_valid, w_qkv, w_out, w_act, class_table, cam_bias):
        args = (tokens, frame_valid, w_qkv, w_out, w_act, class_table, cam_bias)
        powers = all(n & (n - 1) == 0 for n in (fsdp, seq)) and fsdp >= 4 and seq >= 2
        aligned = w_qkv.shape[0] % (fsdp * LANES) == 0 and w_qkv.shape[2] % (seq * 2 * DH) == 0
        one_window = tokens.shape[0] == mesh.shape["groups"] * fsdp
        one_window = one_window and tokens.shape[1] == mesh.shape["sub"] and tokens.shape[2] == seq
        one = make(mesh) if powers and aligned and one_window else plain
        in_specs = (
            P(("groups", "fsdp"), "sub", "seq", None, None),
            P(("groups", "fsdp"), "sub", None),
            P("fsdp", None, "seq"),
            P("seq", "fsdp"),
            P(None, "fsdp"),
            P("fsdp"),
            P(),
        )
        out_specs = (
            P(("groups", "fsdp"), "sub", "seq", None, None),
            P("groups", "sub", "seq", "fsdp"),
        )
        run = jax.shard_map(
            one, mesh=mesh, in_specs=in_specs, out_specs=out_specs, check_vma=False
        )
        return run(*args)

    return whole
```

```python
import functools
import math

import jax
import jax.numpy as jnp
from jax import lax
from jax.experimental import pallas as pl
from jax.experimental.pallas import tpu as pltpu
from jax.sharding import PartitionSpec as P

DH = 128
LANES = 128
F32 = jnp.float32
BF16 = jnp.bfloat16
VMEM = pl.BlockSpec(memory_space=pltpu.VMEM)
SMEM = pl.BlockSpec(memory_space=pltpu.SMEM)
WINDOW = 4
PARAMS = pltpu.CompilerParams(vmem_limit_bytes=16 * 2**20)


def normalize(values):
    centre = jnp.mean(values, axis=-1, keepdims=True)
    spread = jnp.mean(jnp.square(values - centre), axis=-1, keepdims=True)
    return (values - centre) * lax.rsqrt(spread + 1e-05)


def after(value, *done):
    return lax.optimization_barrier((value, *done))[0]


def cost(flops, size):
    return pl.CostEstimate(flops=flops, bytes_accessed=size, transcendentals=0)


def ring_place(index, n):
    return index // 2 if index % 2 == 0 else n - 1 - index // 2


def owners(distances):
    n = len(distances)
    me = lax.axis_index("fsdp")
    half = lax.shift_right_logical(me, 1)
    place = jnp.where((me & 1) == 0, half, n - 1 - half)
    found = []
    for distance in distances:
        at = lax.rem(place + (distance + n), n)
        found.append(jnp.where(at < n // 2, 2 * at, 2 * (n - at) - 1))
    return found


def norm_kernel(distances, tokens_ref, normed_ref, mean_ref):
    values = tokens_ref[...].astype(F32)
    width = values.shape[1]
    centre = jnp.mean(values, axis=1, keepdims=True)
    spread = jnp.mean(jnp.square(values - centre), axis=1, keepdims=True)
    scale = lax.rsqrt(spread + 1e-05)
    mean = jnp.mean(values, axis=0, keepdims=True)
    columns = mean_ref.shape[1]
    for i in range(mean_ref.shape[0]):
        mean_ref[i : i + 1, :] = mean[:, i * columns : (i + 1) * columns]
    block = width // len(distances)
    for i, owner in enumerate(owners(distances)):
        at = pl.multiple_of(owner * block, LANES)
        piece = tokens_ref[:, pl.ds(at, block)].astype(F32)
        normed_ref[:, i * block : (i + 1) * block] = ((piece - centre) * scale).astype(BF16)


def norm_call(distances, tokens, columns):
    rows, width = tokens.shape
    return pl.pallas_call(
        functools.partial(norm_kernel, distances),
        out_shape=(
            jax.ShapeDtypeStruct((rows, width), BF16),
            jax.ShapeDtypeStruct((width // columns, columns), F32),
        ),
        in_specs=[VMEM],
        out_specs=(VMEM, VMEM),
        compiler_params=PARAMS,
        cost_estimate=cost(8 * rows * width, 4 * rows * width),
        name="norm",
    )(tokens)


def fetch(sources, buffers, sems):
    copies = [
        pltpu.make_async_copy(source, buffer, sems.at[i])
        for i, (source, buffer) in enumerate(zip(sources, buffers))
    ]
    for copy in copies:
        copy.start()

    def get(i):
        copies[i].wait()
        return buffers[i][...]

    return get


def frames_of(refs):
    return [(ref, frame) for ref in refs for frame in range(ref.shape[0])]


def times_rows(sources, first, blocks, total):
    at = first
    for block in blocks:
        depth = block.shape[0]
        rows = [ref[frame, :, at : at + depth] for ref, frame in frames_of(sources)]
        term = jnp.dot(jnp.concatenate(rows, axis=0), block, preferred_element_type=F32)
        total = term if total is None else total + term
        at += depth
    return total


def early_kernel(tensors, own_ref, core_ref, *refs):
    count = (len(refs) - 2) // 2
    sources, out_ref = refs[:count], refs[count]
    buffers, sems = refs[count + 1 : -1], refs[-1]
    get = fetch(sources, buffers, sems)
    for tensor in range(tensors):
        blocks = [get(i) for i in range(tensor, count, tensors)]
        out_ref[tensor] = times_rows((own_ref, core_ref), 0, blocks, None)


ANY = pl.BlockSpec(memory_space=pltpu.HBM)


def scratch_for(blocks):
    return [pltpu.VMEM(b.shape, b.dtype) for b in blocks] + [pltpu.SemaphoreType.DMA((len(blocks),))]


def early_call(tokens, blocks, tensors):
    rows = 2 * tokens[0].shape[0] * tokens[0].shape[1]
    columns = blocks[0].shape[1]
    depth = sum(b.shape[0] for b in blocks)
    return pl.pallas_call(
        functools.partial(early_kernel, tensors),
        out_shape=jax.ShapeDtypeStruct((tensors, rows, columns), F32),
        in_specs=[VMEM] * 2 + [ANY] * len(blocks),
        out_specs=VMEM,
        scratch_shapes=scratch_for(blocks),
        compiler_params=PARAMS,
        cost_estimate=cost(2 * rows * columns * depth, 2 * columns * depth),
        name="early",
    )(*tokens, *blocks)


def late_kernel(counts, first, own_ref, core_ref, part_ref, *refs):
    count = sum(counts)
    sources, outs = refs[:count], refs[count : count + len(counts)]
    buffers, sems = refs[count + len(counts) : -1], refs[-1]
    get = fetch(sources, buffers, sems)
    at = 0
    for tensor, number in enumerate(counts):
        blocks = [get(at + i) for i in range(number)]
        at += number
        total = times_rows((own_ref, core_ref), first, blocks, part_ref[tensor])
        outs[tensor][...] = total.astype(BF16)


def late_call(tokens, part, blocks):
    flat = [b for tensor in blocks for b in tensor]
    rows, columns = part.shape[1], part.shape[2]
    depth = sum(b.shape[0] for b in flat)
    first = tokens[0].shape[2] - sum(b.shape[0] for b in blocks[0])
    shape = jax.ShapeDtypeStruct((rows, columns), BF16)
    return pl.pallas_call(
        functools.partial(late_kernel, [len(b) for b in blocks], first),
        out_shape=[shape] * len(blocks),
        in_specs=[VMEM] * 3 + [ANY] * len(flat),
        out_specs=[VMEM] * len(blocks),
        scratch_shapes=scratch_for(flat),
        compiler_params=PARAMS,
        cost_estimate=cost(2 * rows * columns * depth, 2 * columns * depth),
        name="late",
    )(*tokens, part, *flat)


def attend_kernel(first, slots, valid_ref, mean_ref, own_ref, core_ref, part_ref, q_ref, k_ref, *refs):
    count = (len(refs) - 3) // 2
    mixed_ref, means_ref = refs[count : count + 2]
    get = fetch(refs[:count], refs[count + 2 : -1], refs[-1])
    scale = 1.0 / math.sqrt(DH)
    rows = own_ref.shape[1]
    frames = mixed_ref.shape[0] // rows
    means_ref[0, frames:, :] = mean_ref[...]
    me = lax.axis_index("seq")
    flags = [valid_ref[me ^ slot].astype(F32) for slot in slots]
    mask = jnp.concatenate([jnp.full((1, rows), flag, F32) for flag in flags], axis=1)
    blocks = [get(i) for i in range(count)]
    v = times_rows((own_ref, core_ref), first, blocks, part_ref[part_ref.shape[0] - 1]).astype(BF16)
    for head in range(v.shape[1] // DH):
        at = slice(head * DH, (head + 1) * DH)
        scores = lax.dot_general(
            q_ref[:, at], k_ref[:, at], (((1,), (1,)), ((), ())), preferred_element_type=F32
        )
        weights = jnp.exp(scores * scale) * mask
        totals = jnp.sum(weights, axis=1, keepdims=True)
        mixed = jnp.dot(weights.astype(BF16), v[:, at], preferred_element_type=F32)
        mixed = (mixed / totals).astype(BF16)
        mixed_ref[:, at] = mixed
        for frame in range(frames):
            part = mixed[frame * rows : (frame + 1) * rows].astype(F32)
            means_ref[0, frame : frame + 1, at] = jnp.mean(part, axis=0, keepdims=True)


def attend_call(slots, valid, token_mean, tokens, part, q, k, blocks):
    rows, columns = q.shape
    depth = tokens[0].shape[2]
    means = rows // tokens[0].shape[1] + token_mean.shape[0]
    first = depth - sum(b.shape[0] for b in blocks)
    return pl.pallas_call(
        functools.partial(attend_kernel, first, slots),
        out_shape=(
            jax.ShapeDtypeStruct((rows, columns), BF16),
            jax.ShapeDtypeStruct((1, means, columns), F32),
        ),
        in_specs=[SMEM] + [VMEM] * 6 + [ANY] * len(blocks),
        out_specs=(VMEM, VMEM),
        scratch_shapes=scratch_for(blocks),
        compiler_params=PARAMS,
        cost_estimate=cost(2 * rows * columns * (depth + 2 * rows), 2 * columns * depth),
        name="attend",
    )(valid, token_mean, *tokens, part, q, k, *blocks)


def times_block(values, parts):
    total, at = None, 0
    for part in parts:
        term = jnp.dot(values[:, at : at + part.shape[0]], part[...], preferred_element_type=F32)
        total = term if total is None else total + term
        at += part.shape[0]
    return total


def out_kernel(counts, mixed_ref, *refs):
    blocks, at = [], 0
    for count in counts:
        blocks.append(refs[at : at + count])
        at += count
    send_ref, keep_ref = refs[at:]
    half = mixed_ref.shape[0] // 2
    columns = blocks[0][0].shape[1]
    for i, parts in enumerate(blocks):
        result = times_block(mixed_ref, parts)
        keep_ref[:, i * columns : (i + 1) * columns] = result[:half]
        send_ref[:, i * columns : (i + 1) * columns] = result[half:].astype(BF16)


def out_call(mixed, blocks):
    flat = [part for parts in blocks for part in parts]
    rows, depth = mixed.shape
    columns = len(blocks) * blocks[0][0].shape[1]
    return pl.pallas_call(
        functools.partial(out_kernel, [len(parts) for parts in blocks]),
        out_shape=(
            jax.ShapeDtypeStruct((rows // 2, columns), BF16),
            jax.ShapeDtypeStruct((rows // 2, columns), F32),
        ),
        in_specs=[VMEM] * (1 + len(flat)),
        out_specs=(VMEM, VMEM),
        compiler_params=PARAMS,
        cost_estimate=cost(2 * rows * columns * depth, 2 * depth * columns + 6 * rows * columns),
        name="out",
    )(mixed, *flat)


def pool_kernel(counts, frames, means_ref, *refs):
    blocks, at = [], 0
    for count in counts:
        blocks.append(refs[at : at + count])
        at += count
    send_ref, keep_ref, held = refs[at:]
    windows = means_ref.shape[0]
    rows = windows * frames
    for r in range(windows):
        for frame in range(frames):
            to = frame * windows + r
            held[to : to + 1, :] = means_ref[r, frame : frame + 1, :]
    values = held[...]
    upper = values.astype(BF16)
    lower = (values - upper.astype(F32)).astype(BF16)
    both = jnp.concatenate([upper, lower], axis=0)
    columns = blocks[0][0].shape[1]
    for i, parts in enumerate(blocks):
        result = times_block(both, parts)
        result = result[:rows] + result[rows:]
        keep_ref[:, i * columns : (i + 1) * columns] = result[: rows // 2]
        send_ref[:, i * columns : (i + 1) * columns] = result[rows // 2 :]


def pool_call(means, blocks, frames):
    flat = [part for parts in blocks for part in parts]
    rows, depth = frames * means.shape[0], means.shape[2]
    columns = len(blocks) * blocks[0][0].shape[1]
    shape = jax.ShapeDtypeStruct((rows // 2, columns), F32)
    return pl.pallas_call(
        functools.partial(pool_kernel, [len(parts) for parts in blocks], frames),
        out_shape=(shape, shape),
        in_specs=[VMEM] * (1 + len(flat)),
        out_specs=(VMEM, VMEM),
        scratch_shapes=[pltpu.VMEM((rows, depth), F32)],
        compiler_params=PARAMS,
        cost_estimate=cost(4 * rows * columns * depth, 2 * depth * columns),
        name="pool",
    )(means, *flat)


def finish_kernel(distances, groups, tokens_ref, *refs):
    out_ref = refs[-1]
    rows = tokens_ref.shape[0]
    slot = 0
    block = tokens_ref.shape[1] // len(distances)
    found = owners(distances)
    for g in range(groups):
        sums, came = refs[2 * g], refs[2 * g + 1]
        for i in range(sums.shape[1] // block):
            at = pl.ds(pl.multiple_of(found[slot] * block, LANES), block)
            here = slice(i * block, (i + 1) * block)
            total = sums[:rows, here] + came[:, here].astype(F32)
            out_ref[:, at] = (tokens_ref[:, at].astype(F32) + total).astype(BF16)
            slot += 1


def finish_call(distances, tokens, sums):
    flat = [part for pair in sums for part in pair]
    return pl.pallas_call(
        functools.partial(finish_kernel, distances, len(sums)),
        out_shape=jax.ShapeDtypeStruct(tokens.shape, BF16),
        in_specs=[VMEM] * (1 + len(flat)),
        out_specs=VMEM,
        compiler_params=PARAMS,
        cost_estimate=cost(4 * tokens.size, 10 * tokens.size),
        name="finish",
    )(tokens, *flat)


def head_kernel(distances, slots, sums_ref, came_ref, means_ref, act_ref, bias_ref, out_ref, pooled):
    windows, width = pooled.shape
    columns = means_ref.shape[2]
    first = means_ref.shape[1] - width // columns
    for i in range(width // columns):
        pooled[:, i * columns : (i + 1) * columns] = means_ref[:, first + i, :]
    block = width // len(distances)
    for i, owner in enumerate(owners(distances)):
        at = pl.ds(pl.multiple_of(owner * block, LANES), block)
        here = slice(i * block, (i + 1) * block)
        pooled[:, at] += sums_ref[:windows, here] + came_ref[:, here]
    values = normalize(pooled[...]).astype(BF16)
    logits = jnp.dot(values, act_ref[...], preferred_element_type=F32) + bias_ref[...]
    me = lax.axis_index("fsdp")
    for i, slot in enumerate(slots):
        out_ref[pl.ds(me ^ slot, 1), 0, 0, :] = logits[i : i + 1]


def head_call(distances, slots, sums, came, means, act, bias):
    width, columns = act.shape
    return pl.pallas_call(
        functools.partial(head_kernel, distances, slots),
        out_shape=jax.ShapeDtypeStruct((means.shape[0], 1, 1, columns), F32),
        in_specs=[VMEM] * 5,
        out_specs=VMEM,
        scratch_shapes=[pltpu.VMEM((means.shape[0], width), F32)],
        compiler_params=PARAMS,
        cost_estimate=cost(2 * means.shape[0] * act.size, 2 * act.size),
        name="head",
    )(sums, came, means, act, bias)


def make(mesh):
    fsdp, seq = mesh.shape["fsdp"], mesh.shape["seq"]
    order = sorted(range(fsdp), key=lambda i: ring_place(i, fsdp))
    forward = [(order[i], order[(i + 1) % fsdp]) for i in range(fsdp)]
    backward = [(b, a) for a, b in forward]
    wide_bits = [1 << i for i in range(1, (seq - 1).bit_length())]
    distances = [0]
    for t in range(1, fsdp // 2):
        distances += [-t, t]
    distances.append(fsdp // 2)

    def over_fsdp(value, bit):
        return lax.ppermute(value, "fsdp", [(i, i ^ bit) for i in range(fsdp)])

    def over_seq(value, bit):
        return lax.ppermute(value, "seq", [(i, i ^ bit) for i in range(seq)])

    def per_device(tokens, frame_valid, w_qkv, w_out, w_act, class_table, cam_bias):
        frame_rows, width = tokens.shape[3], tokens.shape[4]
        own_tokens = tokens.reshape(frame_rows, width)
        by_tensor = jnp.transpose(w_qkv, (1, 0, 2))
        sent = []
        first = by_tensor[0]
        others = after(by_tensor, first)
        chains = {"q": first, "k": others[1], "v": others[2], "o": w_out}
        edge = {name: [start, start] for name, start in chains.items()}
        came = {name: [start] for name, start in chains.items()}

        def move(name, way):
            value = edge[name][way]
            if len(sent) >= WINDOW:
                value = after(value, sent[-WINDOW])
            value = lax.ppermute(value, "fsdp", backward if way else forward)
            edge[name][way] = value
            came[name].append(value)
            sent.append(value)

        def both(name):
            move(name, 0)
            move(name, 1)

        normed, token_mean = norm_call(distances, own_tokens, w_qkv.shape[2])
        own = normed[None]
        frame_slots = [0]
        for bit in wide_bits:
            own = jnp.concatenate([own, over_seq(own, bit)], axis=0)
            frame_slots = frame_slots + [o ^ bit for o in frame_slots]
        frame_slots = frame_slots + [o ^ 1 for o in frame_slots]

        steps = fsdp // 2
        soon = 2 if steps > 2 else 1
        for _ in range(soon):
            for name in "qkv":
                both(name)
        count = 2 * soon + 1
        rows = (own, over_seq(own, 1))
        part = early_call(rows, [came[name][i] for i in range(count) for name in "qkv"], 3)
        for _ in range(soon, steps - 1):
            for name in "qkv":
                both(name)
        both("o")
        move("q", 0)
        move("k", 1)
        move("v", 0)
        for _ in range(1, steps - 1):
            move("o", 1)
            move("o", 0)
            came["o"][-2:] = came["o"][:-3:-1]

        qkv, blocks = [came[name] for name in "qkv"], [[block] for block in came["o"]]

        q, k = late_call(rows, part, [qkv[0][count:], qkv[1][count:]])
        mixed, means = attend_call(
            frame_slots, frame_valid.reshape(seq), token_mean, rows, part, q, k, qkv[2][count:]
        )

        def reduce_once(keep, arrived, to):
            total = keep + arrived.astype(F32)
            half = total.shape[0] // 2
            return total[:half], total[half:].astype(to)

        def reduce_all(send, keep, to, *done):
            crossed = arrived = over_seq(send, 1)
            for bit in wide_bits[::-1]:
                keep, leave = reduce_once(keep, arrived, to)
                arrived = over_seq(after(leave, *done) if done else leave, bit)
            return keep, arrived, crossed

        windows = [0]
        bits = [1 << i for i in range((fsdp - 1).bit_length())][::-1]
        seen = []

        def gather(means, bit, *done):
            seen.append(over_fsdp(after(means, *done) if done else means, bit))
            windows.extend([window ^ bit for window in windows])
            return jnp.concatenate([means, seen[-1]], axis=0)

        cut = min(5, len(blocks) - 1)
        near = [block for (block,) in blocks[cut:]]
        *early, crossed = reduce_all(*out_call(mixed, blocks[:cut]), BF16)
        means = gather(means, bits[0])
        edge["o"][1] = after(edge["o"][1], crossed)
        move("o", 1)
        blocks.append([came["o"][-1]])
        waits = {1: (crossed,), 2: (early[1],)}
        for i, bit in enumerate(bits[1:], 1):
            means = gather(means, bit, *waits.get(i, ()))

        pool_keep, pool_came, _ = reduce_all(*pool_call(after(means, early[1]), blocks, seq), F32)
        later = reduce_all(*out_call(after(mixed, means), blocks[cut:]), BF16)
        sums = [early, later[:2]]
        hidden = finish_call(distances, own_tokens, sums)

        camera_ids = jnp.arange(cam_bias.shape[0], dtype=jnp.int32)
        onehot = (class_table[:, None] == camera_ids[None, :]).astype(F32)
        bias = jnp.dot(onehot, cam_bias, precision=lax.Precision.HIGHEST)[None]
        logits = head_call(distances, windows, pool_keep, pool_came, means, w_act, bias)
        return hidden.reshape(tokens.shape), logits

    return per_device


def plain(tokens, frame_valid, w_qkv, w_out, w_act, class_table, cam_bias):
    windows_here, frame_rows, width = tokens.shape[0], tokens.shape[3], tokens.shape[4]
    own_rows = tokens[:, 0, 0].astype(F32)
    normed = normalize(own_rows).astype(BF16)
    gathered = lax.all_gather(normed[:, None], "seq", axis=1, tiled=True)
    frame_count = gathered.shape[1]
    span = frame_count * frame_rows
    rows = gathered.reshape(windows_here, span, width)
    full_qkv = lax.all_gather(w_qkv, "fsdp", axis=0, tiled=True)
    projected = jnp.einsum("wsd,dcn->wscn", rows, full_qkv, preferred_element_type=F32)
    heads = full_qkv.shape[2] // DH
    projected = projected.astype(BF16).reshape(windows_here, span, 3, heads, DH)
    q, k, v = projected[:, :, 0], projected[:, :, 1], projected[:, :, 2]
    key_mask = jnp.repeat(frame_valid[:, 0].astype(F32), frame_rows, axis=1)
    scores = jnp.einsum("wqhe,wkhe->whqk", q, k, preferred_element_type=F32) / math.sqrt(DH)
    weights = jnp.exp(scores) * key_mask[:, None, None, :]
    totals = jnp.sum(weights, axis=-1)
    mixed = jnp.einsum("whqk,wkhe->wqhe", weights.astype(BF16), v, preferred_element_type=F32)
    mixed = (mixed / jnp.transpose(totals, (0, 2, 1))[:, :, :, None]).astype(BF16)
    mixed = mixed.reshape(windows_here, frame_count, frame_rows, heads * DH)
    mixed = jnp.transpose(mixed, (1, 0, 2, 3)).reshape(-1, heads * DH)
    full_out = lax.all_gather(w_out, "fsdp", axis=1, tiled=True)
    branch = lax.psum_scatter(
        jnp.dot(mixed, full_out, preferred_element_type=F32), "seq", scatter_dimension=0, tiled=True
    )
    hidden = (own_rows + branch.reshape(windows_here, frame_rows, width)).astype(BF16)
    wide = lax.optimization_barrier(hidden).astype(F32)
    pooled = normalize(jnp.mean(wide, axis=1)).astype(BF16)
    camera_ids = jnp.arange(cam_bias.shape[0], dtype=jnp.int32)
    onehot = (class_table[:, None] == camera_ids[None, :]).astype(F32)
    bias = jnp.dot(onehot, cam_bias, precision=lax.Precision.HIGHEST)
    everywhere = lax.all_gather(pooled, "fsdp", axis=0, tiled=True)
    logits = jnp.dot(everywhere, w_act, preferred_element_type=F32) + bias[None, :]
    return (
        hidden.reshape(windows_here, 1, 1, frame_rows, width),
        logits.reshape(logits.shape[0], 1, 1, logits.shape[1]),
    )


def solution(mesh):
    fsdp, seq = mesh.shape["fsdp"], mesh.shape["seq"]

    def whole(tokens, frame_valid, w_qkv, w_out, w_act, class_table, cam_bias):
        args = (tokens, frame_valid, w_qkv, w_out, w_act, class_table, cam_bias)
        powers = all(n & (n - 1) == 0 for n in (fsdp, seq)) and fsdp >= 4 and seq >= 2
        aligned = w_qkv.shape[0] % (fsdp * LANES) == 0 and w_qkv.shape[2] % (seq * 2 * DH) == 0
        one_window = tokens.shape[0] == mesh.shape["groups"] * fsdp
        one_window = one_window and tokens.shape[1] == mesh.shape["sub"] and tokens.shape[2] == seq
        one = make(mesh) if powers and aligned and one_window else plain
        in_specs = (
            P(("groups", "fsdp"), "sub", "seq", None, None),
            P(("groups", "fsdp"), "sub", None),
            P("fsdp", None, "seq"),
            P("seq", "fsdp"),
            P(None, "fsdp"),
            P("fsdp"),
            P(),
        )
        out_specs = (
            P(("groups", "fsdp"), "sub", "seq", None, None),
            P("groups", "sub", "seq", "fsdp"),
        )
        run = jax.shard_map(
            one, mesh=mesh, in_specs=in_specs, out_specs=out_specs, check_vma=False
        )
        return run(*args)

    return whole
```

```python
import functools
import math

import jax
import jax.numpy as jnp
from jax import lax
from jax.experimental import pallas as pl
from jax.experimental.pallas import tpu as pltpu
from jax.sharding import PartitionSpec as P

DH = 128
LANES = 128
F32 = jnp.float32
BF16 = jnp.bfloat16
VMEM = pl.BlockSpec(memory_space=pltpu.VMEM)
SMEM = pl.BlockSpec(memory_space=pltpu.SMEM)
WINDOW = 4
PARAMS = pltpu.CompilerParams(vmem_limit_bytes=16 * 2**20)


def normalize(values):
    centre = jnp.mean(values, axis=-1, keepdims=True)
    spread = jnp.mean(jnp.square(values - centre), axis=-1, keepdims=True)
    return (values - centre) * lax.rsqrt(spread + 1e-05)


def after(value, *done):
    return lax.optimization_barrier((value, *done))[0]


def cost(flops, size):
    return pl.CostEstimate(flops=flops, bytes_accessed=size, transcendentals=0)


def ring_place(index, n):
    return index // 2 if index % 2 == 0 else n - 1 - index // 2


def owners(distances):
    n = len(distances)
    me = lax.axis_index("fsdp")
    half = lax.shift_right_logical(me, 1)
    place = jnp.where((me & 1) == 0, half, n - 1 - half)
    found = []
    for distance in distances:
        at = lax.rem(place + (distance + n), n)
        found.append(jnp.where(at < n // 2, 2 * at, 2 * (n - at) - 1))
    return found


def norm_kernel(distances, tokens_ref, normed_ref, mean_ref):
    values = tokens_ref[...].astype(F32)
    width = values.shape[1]
    centre = jnp.mean(values, axis=1, keepdims=True)
    spread = jnp.mean(jnp.square(values - centre), axis=1, keepdims=True)
    scale = lax.rsqrt(spread + 1e-05)
    mean = jnp.mean(values, axis=0, keepdims=True)
    columns = mean_ref.shape[1]
    for i in range(mean_ref.shape[0]):
        mean_ref[i : i + 1, :] = mean[:, i * columns : (i + 1) * columns]
    block = width // len(distances)
    for i, owner in enumerate(owners(distances)):
        at = pl.multiple_of(owner * block, LANES)
        piece = tokens_ref[:, pl.ds(at, block)].astype(F32)
        normed_ref[:, i * block : (i + 1) * block] = ((piece - centre) * scale).astype(BF16)


def norm_call(distances, tokens, columns):
    rows, width = tokens.shape
    return pl.pallas_call(
        functools.partial(norm_kernel, distances),
        out_shape=(
            jax.ShapeDtypeStruct((rows, width), BF16),
            jax.ShapeDtypeStruct((width // columns, columns), F32),
        ),
        in_specs=[VMEM],
        out_specs=(VMEM, VMEM),
        compiler_params=PARAMS,
        cost_estimate=cost(8 * rows * width, 4 * rows * width),
        name="norm",
    )(tokens)


def fetch(sources, buffers, sems):
    copies = [
        pltpu.make_async_copy(source, buffer, sems.at[i])
        for i, (source, buffer) in enumerate(zip(sources, buffers))
    ]
    for copy in copies:
        copy.start()

    def get(i):
        copies[i].wait()
        return buffers[i][...]

    return get


def frames_of(refs):
    return [(ref, frame) for ref in refs for frame in range(ref.shape[0])]


def times_rows(sources, first, blocks, total):
    at = first
    for block in blocks:
        depth = block.shape[0]
        rows = [ref[frame, :, at : at + depth] for ref, frame in frames_of(sources)]
        term = jnp.dot(jnp.concatenate(rows, axis=0), block, preferred_element_type=F32)
        total = term if total is None else total + term
        at += depth
    return total


def early_kernel(tensors, own_ref, core_ref, *refs):
    count = (len(refs) - 2) // 2
    sources, out_ref = refs[:count], refs[count]
    buffers, sems = refs[count + 1 : -1], refs[-1]
    get = fetch(sources, buffers, sems)
    for tensor in range(tensors):
        blocks = [get(i) for i in range(tensor, count, tensors)]
        out_ref[tensor] = times_rows((own_ref, core_ref), 0, blocks, None)


ANY = pl.BlockSpec(memory_space=pltpu.HBM)


def scratch_for(blocks):
    return [pltpu.VMEM(b.shape, b.dtype) for b in blocks] + [pltpu.SemaphoreType.DMA((len(blocks),))]


def early_call(tokens, blocks, tensors):
    rows = 2 * tokens[0].shape[0] * tokens[0].shape[1]
    columns = blocks[0].shape[1]
    depth = sum(b.shape[0] for b in blocks)
    return pl.pallas_call(
        functools.partial(early_kernel, tensors),
        out_shape=jax.ShapeDtypeStruct((tensors, rows, columns), F32),
        in_specs=[VMEM] * 2 + [ANY] * len(blocks),
        out_specs=VMEM,
        scratch_shapes=scratch_for(blocks),
        compiler_params=PARAMS,
        cost_estimate=cost(2 * rows * columns * depth, 2 * columns * depth),
        name="early",
    )(*tokens, *blocks)


def late_kernel(counts, first, own_ref, core_ref, part_ref, *refs):
    count = sum(counts)
    sources, outs = refs[:count], refs[count : count + len(counts)]
    buffers, sems = refs[count + len(counts) : -1], refs[-1]
    get = fetch(sources, buffers, sems)
    at = 0
    for tensor, number in enumerate(counts):
        blocks = [get(at + i) for i in range(number)]
        at += number
        total = times_rows((own_ref, core_ref), first, blocks, part_ref[tensor])
        outs[tensor][...] = total.astype(BF16)


def late_call(tokens, part, blocks):
    flat = [b for tensor in blocks for b in tensor]
    rows, columns = part.shape[1], part.shape[2]
    depth = sum(b.shape[0] for b in flat)
    first = tokens[0].shape[2] - sum(b.shape[0] for b in blocks[0])
    shape = jax.ShapeDtypeStruct((rows, columns), BF16)
    return pl.pallas_call(
        functools.partial(late_kernel, [len(b) for b in blocks], first),
        out_shape=[shape] * len(blocks),
        in_specs=[VMEM] * 3 + [ANY] * len(flat),
        out_specs=[VMEM] * len(blocks),
        scratch_shapes=scratch_for(flat),
        compiler_params=PARAMS,
        cost_estimate=cost(2 * rows * columns * depth, 2 * columns * depth),
        name="late",
    )(*tokens, part, *flat)


def attend_kernel(first, slots, valid_ref, mean_ref, own_ref, core_ref, part_ref, q_ref, k_ref, *refs):
    count = (len(refs) - 3) // 2
    mixed_ref, means_ref = refs[count : count + 2]
    get = fetch(refs[:count], refs[count + 2 : -1], refs[-1])
    scale = 1.0 / math.sqrt(DH)
    rows = own_ref.shape[1]
    frames = mixed_ref.shape[0] // rows
    means_ref[0, frames:, :] = mean_ref[...]
    me = lax.axis_index("seq")
    flags = [valid_ref[me ^ slot].astype(F32) for slot in slots]
    mask = jnp.concatenate([jnp.full((1, rows), flag, F32) for flag in flags], axis=1)
    blocks = [get(i) for i in range(count)]
    v = times_rows((own_ref, core_ref), first, blocks, part_ref[part_ref.shape[0] - 1]).astype(BF16)
    for head in range(v.shape[1] // DH):
        at = slice(head * DH, (head + 1) * DH)
        scores = lax.dot_general(
            q_ref[:, at], k_ref[:, at], (((1,), (1,)), ((), ())), preferred_element_type=F32
        )
        weights = jnp.exp(scores * scale) * mask
        totals = jnp.sum(weights, axis=1, keepdims=True)
        mixed = jnp.dot(weights.astype(BF16), v[:, at], preferred_element_type=F32)
        mixed = (mixed / totals).astype(BF16)
        mixed_ref[:, at] = mixed
        for frame in range(frames):
            part = mixed[frame * rows : (frame + 1) * rows].astype(F32)
            means_ref[0, frame : frame + 1, at] = jnp.mean(part, axis=0, keepdims=True)


def attend_call(slots, valid, token_mean, tokens, part, q, k, blocks):
    rows, columns = q.shape
    depth = tokens[0].shape[2]
    means = rows // tokens[0].shape[1] + token_mean.shape[0]
    first = depth - sum(b.shape[0] for b in blocks)
    return pl.pallas_call(
        functools.partial(attend_kernel, first, slots),
        out_shape=(
            jax.ShapeDtypeStruct((rows, columns), BF16),
            jax.ShapeDtypeStruct((1, means, columns), F32),
        ),
        in_specs=[SMEM] + [VMEM] * 6 + [ANY] * len(blocks),
        out_specs=(VMEM, VMEM),
        scratch_shapes=scratch_for(blocks),
        compiler_params=PARAMS,
        cost_estimate=cost(2 * rows * columns * (depth + 2 * rows), 2 * columns * depth),
        name="attend",
    )(valid, token_mean, *tokens, part, q, k, *blocks)


def times_block(values, parts):
    total, at = None, 0
    for part in parts:
        term = jnp.dot(values[:, at : at + part.shape[0]], part[...], preferred_element_type=F32)
        total = term if total is None else total + term
        at += part.shape[0]
    return total


def out_kernel(counts, mixed_ref, *refs):
    blocks, at = [], 0
    for count in counts:
        blocks.append(refs[at : at + count])
        at += count
    send_ref, keep_ref = refs[at:]
    half = mixed_ref.shape[0] // 2
    columns = blocks[0][0].shape[1]
    for i, parts in enumerate(blocks):
        result = times_block(mixed_ref, parts)
        keep_ref[:, i * columns : (i + 1) * columns] = result[:half]
        send_ref[:, i * columns : (i + 1) * columns] = result[half:].astype(BF16)


def out_call(mixed, blocks):
    flat = [part for parts in blocks for part in parts]
    rows, depth = mixed.shape
    columns = len(blocks) * blocks[0][0].shape[1]
    return pl.pallas_call(
        functools.partial(out_kernel, [len(parts) for parts in blocks]),
        out_shape=(
            jax.ShapeDtypeStruct((rows // 2, columns), BF16),
            jax.ShapeDtypeStruct((rows // 2, columns), F32),
        ),
        in_specs=[VMEM] * (1 + len(flat)),
        out_specs=(VMEM, VMEM),
        compiler_params=PARAMS,
        cost_estimate=cost(2 * rows * columns * depth, 2 * depth * columns + 6 * rows * columns),
        name="out",
    )(mixed, *flat)


def pool_kernel(counts, frames, means_ref, *refs):
    blocks, at = [], 0
    for count in counts:
        blocks.append(refs[at : at + count])
        at += count
    send_ref, keep_ref, held = refs[at:]
    windows = means_ref.shape[0]
    rows = windows * frames
    for r in range(windows):
        for frame in range(frames):
            to = frame * windows + r
            held[to : to + 1, :] = means_ref[r, frame : frame + 1, :]
    values = held[...]
    upper = values.astype(BF16)
    lower = (values - upper.astype(F32)).astype(BF16)
    both = jnp.concatenate([upper, lower], axis=0)
    columns = blocks[0][0].shape[1]
    for i, parts in enumerate(blocks):
        result = times_block(both, parts)
        result = result[:rows] + result[rows:]
        keep_ref[:, i * columns : (i + 1) * columns] = result[: rows // 2]
        send_ref[:, i * columns : (i + 1) * columns] = result[rows // 2 :]


def pool_call(means, blocks, frames):
    flat = [part for parts in blocks for part in parts]
    rows, depth = frames * means.shape[0], means.shape[2]
    columns = len(blocks) * blocks[0][0].shape[1]
    shape = jax.ShapeDtypeStruct((rows // 2, columns), F32)
    return pl.pallas_call(
        functools.partial(pool_kernel, [len(parts) for parts in blocks], frames),
        out_shape=(shape, shape),
        in_specs=[VMEM] * (1 + len(flat)),
        out_specs=(VMEM, VMEM),
        scratch_shapes=[pltpu.VMEM((rows, depth), F32)],
        compiler_params=PARAMS,
        cost_estimate=cost(4 * rows * columns * depth, 2 * depth * columns),
        name="pool",
    )(means, *flat)


def finish_kernel(distances, groups, tokens_ref, *refs):
    out_ref = refs[-1]
    rows = tokens_ref.shape[0]
    slot = 0
    block = tokens_ref.shape[1] // len(distances)
    found = owners(distances)
    for g in range(groups):
        sums, came = refs[2 * g], refs[2 * g + 1]
        for i in range(sums.shape[1] // block):
            at = pl.ds(pl.multiple_of(found[slot] * block, LANES), block)
            here = slice(i * block, (i + 1) * block)
            total = sums[:rows, here] + came[:, here].astype(F32)
            out_ref[:, at] = (tokens_ref[:, at].astype(F32) + total).astype(BF16)
            slot += 1


def finish_call(distances, tokens, sums):
    flat = [part for pair in sums for part in pair]
    return pl.pallas_call(
        functools.partial(finish_kernel, distances, len(sums)),
        out_shape=jax.ShapeDtypeStruct(tokens.shape, BF16),
        in_specs=[VMEM] * (1 + len(flat)),
        out_specs=VMEM,
        compiler_params=PARAMS,
        cost_estimate=cost(4 * tokens.size, 10 * tokens.size),
        name="finish",
    )(tokens, *flat)


def head_kernel(distances, slots, sums_ref, came_ref, means_ref, act_ref, bias_ref, out_ref, pooled):
    windows, width = pooled.shape
    columns = means_ref.shape[2]
    first = means_ref.shape[1] - width // columns
    for i in range(width // columns):
        pooled[:, i * columns : (i + 1) * columns] = means_ref[:, first + i, :]
    block = width // len(distances)
    for i, owner in enumerate(owners(distances)):
        at = pl.ds(pl.multiple_of(owner * block, LANES), block)
        here = slice(i * block, (i + 1) * block)
        pooled[:, at] += sums_ref[:windows, here] + came_ref[:, here]
    values = normalize(pooled[...]).astype(BF16)
    logits = jnp.dot(values, act_ref[...], preferred_element_type=F32) + bias_ref[...]
    me = lax.axis_index("fsdp")
    for i, slot in enumerate(slots):
        out_ref[pl.ds(me ^ slot, 1), 0, 0, :] = logits[i : i + 1]


def head_call(distances, slots, sums, came, means, act, bias):
    width, columns = act.shape
    return pl.pallas_call(
        functools.partial(head_kernel, distances, slots),
        out_shape=jax.ShapeDtypeStruct((means.shape[0], 1, 1, columns), F32),
        in_specs=[VMEM] * 5,
        out_specs=VMEM,
        scratch_shapes=[pltpu.VMEM((means.shape[0], width), F32)],
        compiler_params=PARAMS,
        cost_estimate=cost(2 * means.shape[0] * act.size, 2 * act.size),
        name="head",
    )(sums, came, means, act, bias)


def make(mesh):
    fsdp, seq = mesh.shape["fsdp"], mesh.shape["seq"]
    order = sorted(range(fsdp), key=lambda i: ring_place(i, fsdp))
    forward = [(order[i], order[(i + 1) % fsdp]) for i in range(fsdp)]
    backward = [(b, a) for a, b in forward]
    wide_bits = [1 << i for i in range(1, (seq - 1).bit_length())]
    distances = [0]
    for t in range(1, fsdp // 2):
        distances += [-t, t]
    distances.append(fsdp // 2)

    def over_fsdp(value, bit):
        return lax.ppermute(value, "fsdp", [(i, i ^ bit) for i in range(fsdp)])

    def over_seq(value, bit):
        return lax.ppermute(value, "seq", [(i, i ^ bit) for i in range(seq)])

    def per_device(tokens, frame_valid, w_qkv, w_out, w_act, class_table, cam_bias):
        frame_rows, width = tokens.shape[3], tokens.shape[4]
        own_tokens = tokens.reshape(frame_rows, width)
        by_tensor = jnp.transpose(w_qkv, (1, 0, 2))
        sent = []
        first = by_tensor[0]
        others = after(by_tensor, first)
        chains = {"q": first, "k": others[1], "v": others[2], "o": w_out}
        edge = {name: [start, start] for name, start in chains.items()}
        came = {name: [start] for name, start in chains.items()}

        def move(name, way):
            value = edge[name][way]
            if len(sent) >= WINDOW:
                value = after(value, sent[-WINDOW])
            value = lax.ppermute(value, "fsdp", backward if way else forward)
            edge[name][way] = value
            came[name].append(value)
            sent.append(value)

        def both(name):
            move(name, 0)
            move(name, 1)

        normed, token_mean = norm_call(distances, own_tokens, w_qkv.shape[2])
        own = normed[None]
        frame_slots = [0]
        for bit in wide_bits:
            own = jnp.concatenate([own, over_seq(own, bit)], axis=0)
            frame_slots = frame_slots + [o ^ bit for o in frame_slots]
        frame_slots = frame_slots + [o ^ 1 for o in frame_slots]

        steps = fsdp // 2
        soon = 2 if steps > 2 else 1
        for _ in range(soon):
            for name in "qkv":
                both(name)
        count = 2 * soon + 1
        rows = (own, over_seq(own, 1))
        part = early_call(rows, [came[name][i] for i in range(count) for name in "qkv"], 3)
        for _ in range(soon, steps - 1):
            for name in "qkv":
                both(name)
        both("o")
        move("q", 0)
        move("k", 1)
        move("v", 0)
        for _ in range(1, steps - 1):
            move("o", 1)
            move("o", 0)
            came["o"][-2:] = came["o"][:-3:-1]

        qkv, blocks = [came[name] for name in "qkv"], [[block] for block in came["o"]]

        q, k = late_call(rows, part, [qkv[0][count:], qkv[1][count:]])
        mixed, means = attend_call(
            frame_slots, frame_valid.reshape(seq), token_mean, rows, part, q, k, qkv[2][count:]
        )

        def reduce_once(keep, arrived, to):
            total = keep + arrived.astype(F32)
            half = total.shape[0] // 2
            return total[:half], total[half:].astype(to)

        def reduce_all(send, keep, to, *done):
            crossed = arrived = over_seq(send, 1)
            for bit in wide_bits[::-1]:
                keep, leave = reduce_once(keep, arrived, to)
                arrived = over_seq(after(leave, *done) if done else leave, bit)
            return keep, arrived, crossed

        windows = [0]
        bits = [1 << i for i in range((fsdp - 1).bit_length())][::-1]
        seen = []

        def gather(means, bit, *done):
            seen.append(over_fsdp(after(means, *done) if done else means, bit))
            windows.extend([window ^ bit for window in windows])
            return jnp.concatenate([means, seen[-1]], axis=0)

        cut = min(5, len(blocks) - 1)
        near = [block for (block,) in blocks[cut:]]
        *early, crossed = reduce_all(*out_call(mixed, blocks[:cut]), BF16)
        means = gather(means, bits[0])
        edge["o"][1] = after(edge["o"][1], crossed)
        move("o", 1)
        blocks.append([came["o"][-1]])
        waits = {1: (crossed,), 2: (early[1],)}
        for i, bit in enumerate(bits[1:], 1):
            means = gather(means, bit, *waits.get(i, ()))

        later = reduce_all(*out_call(after(mixed, means), blocks[cut:]), BF16)
        pool_keep, pool_came, _ = reduce_all(*pool_call(after(means, later[2]), blocks, seq), F32)
        sums = [early, later[:2]]
        hidden = finish_call(distances, own_tokens, sums)

        camera_ids = jnp.arange(cam_bias.shape[0], dtype=jnp.int32)
        onehot = (class_table[:, None] == camera_ids[None, :]).astype(F32)
        bias = jnp.dot(onehot, cam_bias, precision=lax.Precision.HIGHEST)[None]
        logits = head_call(distances, windows, pool_keep, pool_came, means, w_act, bias)
        return hidden.reshape(tokens.shape), logits

    return per_device


def plain(tokens, frame_valid, w_qkv, w_out, w_act, class_table, cam_bias):
    windows_here, frame_rows, width = tokens.shape[0], tokens.shape[3], tokens.shape[4]
    own_rows = tokens[:, 0, 0].astype(F32)
    normed = normalize(own_rows).astype(BF16)
    gathered = lax.all_gather(normed[:, None], "seq", axis=1, tiled=True)
    frame_count = gathered.shape[1]
    span = frame_count * frame_rows
    rows = gathered.reshape(windows_here, span, width)
    full_qkv = lax.all_gather(w_qkv, "fsdp", axis=0, tiled=True)
    projected = jnp.einsum("wsd,dcn->wscn", rows, full_qkv, preferred_element_type=F32)
    heads = full_qkv.shape[2] // DH
    projected = projected.astype(BF16).reshape(windows_here, span, 3, heads, DH)
    q, k, v = projected[:, :, 0], projected[:, :, 1], projected[:, :, 2]
    key_mask = jnp.repeat(frame_valid[:, 0].astype(F32), frame_rows, axis=1)
    scores = jnp.einsum("wqhe,wkhe->whqk", q, k, preferred_element_type=F32) / math.sqrt(DH)
    weights = jnp.exp(scores) * key_mask[:, None, None, :]
    totals = jnp.sum(weights, axis=-1)
    mixed = jnp.einsum("whqk,wkhe->wqhe", weights.astype(BF16), v, preferred_element_type=F32)
    mixed = (mixed / jnp.transpose(totals, (0, 2, 1))[:, :, :, None]).astype(BF16)
    mixed = mixed.reshape(windows_here, frame_count, frame_rows, heads * DH)
    mixed = jnp.transpose(mixed, (1, 0, 2, 3)).reshape(-1, heads * DH)
    full_out = lax.all_gather(w_out, "fsdp", axis=1, tiled=True)
    branch = lax.psum_scatter(
        jnp.dot(mixed, full_out, preferred_element_type=F32), "seq", scatter_dimension=0, tiled=True
    )
    hidden = (own_rows + branch.reshape(windows_here, frame_rows, width)).astype(BF16)
    wide = lax.optimization_barrier(hidden).astype(F32)
    pooled = normalize(jnp.mean(wide, axis=1)).astype(BF16)
    camera_ids = jnp.arange(cam_bias.shape[0], dtype=jnp.int32)
    onehot = (class_table[:, None] == camera_ids[None, :]).astype(F32)
    bias = jnp.dot(onehot, cam_bias, precision=lax.Precision.HIGHEST)
    everywhere = lax.all_gather(pooled, "fsdp", axis=0, tiled=True)
    logits = jnp.dot(everywhere, w_act, preferred_element_type=F32) + bias[None, :]
    return (
        hidden.reshape(windows_here, 1, 1, frame_rows, width),
        logits.reshape(logits.shape[0], 1, 1, logits.shape[1]),
    )


def solution(mesh):
    fsdp, seq = mesh.shape["fsdp"], mesh.shape["seq"]

    def whole(tokens, frame_valid, w_qkv, w_out, w_act, class_table, cam_bias):
        args = (tokens, frame_valid, w_qkv, w_out, w_act, class_table, cam_bias)
        powers = all(n & (n - 1) == 0 for n in (fsdp, seq)) and fsdp >= 4 and seq >= 2
        aligned = w_qkv.shape[0] % (fsdp * LANES) == 0 and w_qkv.shape[2] % (seq * 2 * DH) == 0
        one_window = tokens.shape[0] == mesh.shape["groups"] * fsdp
        one_window = one_window and tokens.shape[1] == mesh.shape["sub"] and tokens.shape[2] == seq
        one = make(mesh) if powers and aligned and one_window else plain
        in_specs = (
            P(("groups", "fsdp"), "sub", "seq", None, None),
            P(("groups", "fsdp"), "sub", None),
            P("fsdp", None, "seq"),
            P("seq", "fsdp"),
            P(None, "fsdp"),
            P("fsdp"),
            P(),
        )
        out_specs = (
            P(("groups", "fsdp"), "sub", "seq", None, None),
            P("groups", "sub", "seq", "fsdp"),
        )
        run = jax.shard_map(
            one, mesh=mesh, in_specs=in_specs, out_specs=out_specs, check_vma=False
        )
        return run(*args)

    return whole
```
